32 devices in a mesh: groups: 2 (over y), row: 4 (over x, core), col: 4 (over z).
Axes of the slice: x: 2, y: 2, z: 4, core: 2. Of those that a mesh axis runs over, the one named last changes fastest.
Arguments:
- blocks: bfloat16 [4096, 8192], P('row', 'col'), may hold values from -0.15625 to 0.15625
- tile_map: int32 [8, 16], P('row', 'col'), may hold values from 0 to 1, as said below
- lower_bound: float32 [8192], P('col'), may hold values from -1.5 to -0.2
- upper_bound: float32 [8192], P('col'), may hold values from 0.2 to 1.5
- bound_code: int32 [8192], P('col'), may hold values from 0 to 3
- row_kind: int32 [4096], P('row'), may hold values from 0 to 1
- cost_vector: float32 [8192], P('col'), may hold values from -6 to 6
- right_side: float32 [4096, 512], P('row', 'groups'), parts along dimension 1, may hold values from -6 to 6
- primal_start: float32 [8192, 512], P('col', 'groups'), parts along dimension 1, may hold values from -6 to 6
- dual_start: float32 [4096, 512], P('row', 'groups'), parts along dimension 1, may hold values from -6 to 6
- primal_weight: float32 [512], P('groups'), parts along dimension 0, may hold values from 0.5 to 2
Outputs:
- primal_final: float32 [8192, 512], P('col', 'groups'), parts along dimension 1
- dual_final: float32 [4096, 512], P('row', 'groups'), parts along dimension 1
The draws below stay inside these ranges and needn't reach their ends.
There are 2 independent parts, one for each index of `groups`. The reference program is written for one: setup_inputs(seed, part) draws one part's arguments, and reference() takes and returns one part's arrays. A program takes and returns all parts, laid end to end along the dimension named above; an argument that names none is the same for every part. Nothing has to cross between parts.
Inputs may be any that keep to these rules, and one draw needn't show every extreme that they name: `tile_map`: block row i has its block on the line j = i * 2 nonzero, the blocks one column away from that line mostly nonzero, and few nonzero blocks elsewhere.
All inputs are finite; a program needn't handle non-finite values.
Results may differ from the reference program's by a relative error of at most 0.0025.
Values may be sent and summed in bfloat16 or wider, within the bound.
No kernel may reach another device: no remote copies, remote signals or barrier semaphores. Data moves between devices by JAX's collectives and lax.ppermute only.
A program may use at most 64 MiB of HBM per device.

```python
import math
import jax
import jax.numpy as jnp
from jax import lax

TILE = 512
SCEN = 256
ITERS = 3
M = 4096
N = 8192
MT = 8
NT = 16


def draw_tile_map(key, part):
    key = jax.random.fold_in(key, 11)
    key_near, key_extra = jax.random.split(key)
    rows = jnp.arange(MT, dtype=jnp.int32)[:, None]
    cols = jnp.arange(NT, dtype=jnp.int32)[None, :]
    center = rows * NT // MT
    distance = jnp.abs(cols - center)
    near_draw = jax.random.randint(key_near, (MT, NT), 0, 4) < 3
    extra_draw = jax.random.randint(key_extra, (MT, NT), 0, 16) == 0
    banded = (distance == 0) | (distance <= 1) & near_draw | extra_draw
    return banded.astype(jnp.int32)


def place_ends(values, own_key, smallest, high):
    longest = values.shape.index(max(values.shape))
    spots = []
    for shift in (0, 1):
        where = [jax.random.randint(jax.random.fold_in(own_key, axis), (), 0, length) for axis, length in enumerate(values.shape)]
        where[longest] = (where[longest] + shift) % values.shape[longest]
        spots.append(tuple(where))
    return values.at[spots[0]].set(smallest).at[spots[1]].set(high)


def block_levels(rng, extent, pieces, smallest, largest):
    def one(position, parts):
        heights = jax.random.uniform(jax.random.fold_in(jax.random.fold_in(rng, 6), position), (parts,), jnp.float32, smallest / len(pieces), largest / len(pieces))
        return jnp.repeat(jnp.exp(heights), extent[position] // parts).reshape((-1,) + (1,) * (len(extent) - position - 1))

    gain = one(*pieces[0])
    for cut in pieces[1:]:
        gain = gain * one(*cut)
    return gain


def gaussian(stream_key, shape, spread, limit, cuts=(), kind=jnp.bfloat16):
    array = spread * jax.random.normal(stream_key, shape, jnp.float32)
    if cuts:
        array = array * block_levels(stream_key, shape, cuts, -0.22, 0.18)
    return jnp.clip(array, -limit, limit).astype(kind)


def setup_inputs(seed: int = 0, part: int = 0) -> dict:
    streams_of = jax.random.split(jax.random.key(seed), 12)
    part_keys = jax.random.split(jax.random.fold_in(streams_of[11], part), 12)
    blocks = gaussian(streams_of[0], (M, N), (3 * TILE) ** -0.5, 0.15625, ((0, 4), (1, 4)))
    tile_map = draw_tile_map(jax.random.fold_in(streams_of[11], 71), part)
    lower_bound = jnp.clip(-1.5 + 1.3 * jax.random.uniform(streams_of[2], (N,), jnp.float32) ** block_levels(streams_of[2], (N,), ((0, 4),), -0.2, 0.2), -1.5, -0.2)
    upper_bound = jnp.clip(0.2 + 1.3 * jax.random.uniform(streams_of[3], (N,), jnp.float32) ** block_levels(streams_of[3], (N,), ((0, 4),), -0.2, 0.2), 0.2, 1.5)
    bound_code = place_ends(jax.random.randint(streams_of[4], (N,), 0, 4), jax.random.fold_in(streams_of[4], 1), 0, 3).astype(jnp.int32)
    row_kind = place_ends(jax.random.randint(streams_of[5], (M,), 0, 2), jax.random.fold_in(streams_of[5], 1), 0, 1).astype(jnp.int32)
    cost_vector = gaussian(streams_of[6], (N,), 1.0, 6.0, ((0, 4),), jnp.float32)
    right_side = gaussian(part_keys[7], (M, SCEN), 1.0, 6.0, ((0, 4),), jnp.float32)
    primal_start = gaussian(part_keys[8], (N, SCEN), 1.0, 6.0, ((0, 4),), jnp.float32)
    dual_start = gaussian(part_keys[9], (M, SCEN), 1.0, 6.0, ((0, 4),), jnp.float32)
    primal_weight = jnp.clip(jnp.exp(jax.random.uniform(part_keys[10], (SCEN,), jnp.float32, math.log(0.5), math.log(2.0))), 0.5, 2.0)
    return {"blocks": blocks, "tile_map": tile_map, "lower_bound": lower_bound, "upper_bound": upper_bound, "bound_code": bound_code, "row_kind": row_kind, "cost_vector": cost_vector, "right_side": right_side, "primal_start": primal_start, "dual_start": dual_start, "primal_weight": primal_weight}


step_scale = 0.5

def project_primal(values, lower_bound, upper_bound, bound_code):
    low_on = ((bound_code == 1) | (bound_code == 3))[:, None]
    high_on = ((bound_code == 2) | (bound_code == 3))[:, None]
    values = jnp.where(low_on, jnp.maximum(values, lower_bound[:, None]), values)
    return jnp.where(high_on, jnp.minimum(values, upper_bound[:, None]), values)

def project_dual(values, row_kind):
    return jnp.where((row_kind == 1)[:, None], jnp.maximum(values, 0.0), values)

def apply_forward(bands, col_mask, vector):
    vector_wide = vector.astype(jnp.float32)

    def band_product(band_pair):
        band_rows, mask_row = band_pair
        matrix = band_rows.astype(jnp.float32) * mask_row.astype(jnp.float32)[None, :]
        return jnp.dot(matrix, vector_wide, precision=lax.Precision.HIGHEST)
    result = lax.map(band_product, (bands, col_mask))
    return result.reshape(-1, vector.shape[1])

def apply_back(bands, col_mask, dual_round):
    dual_bands = dual_round.astype(jnp.float32).reshape(bands.shape[0], bands.shape[1], -1)

    def band_step(running, band_pair):
        band_rows, mask_row, dual_rows = band_pair
        matrix = band_rows.astype(jnp.float32) * mask_row.astype(jnp.float32)[None, :]
        return (running + jnp.dot(matrix.T, dual_rows, precision=lax.Precision.HIGHEST), None)
    initial = jnp.zeros((bands.shape[2], dual_round.shape[1]), jnp.float32)
    running, _ = lax.scan(band_step, initial, (bands, col_mask, dual_bands))
    return running

def reference(blocks, tile_map, lower_bound, upper_bound, bound_code, row_kind, cost_vector, right_side, primal_start, dual_start, primal_weight):
    bands = blocks.reshape(MT, TILE, N)
    col_mask = jnp.repeat(tile_map, TILE, axis=1)
    weight_now = primal_weight
    primal = primal_start
    dual = dual_start
    for iteration in range(ITERS):
        primal_step = step_scale / weight_now
        dual_step = step_scale * weight_now
        image_t = apply_back(bands, col_mask, dual.astype(jnp.bfloat16))
        primal_next = project_primal(primal - primal_step[None, :] * (cost_vector[:, None] - image_t), lower_bound, upper_bound, bound_code)
        extrapolated = (2.0 * primal_next - primal).astype(jnp.bfloat16)
        image = apply_forward(bands, col_mask, extrapolated)
        dual_next = project_dual(dual + dual_step[None, :] * (right_side - image), row_kind)
        if iteration + 1 < ITERS:
            move_x = jnp.sqrt(lax.optimization_barrier(jnp.sum((primal_next - primal) ** 2, axis=0)) / N + 1e-06)
            move_y = jnp.sqrt(lax.optimization_barrier(jnp.sum((dual_next - dual) ** 2, axis=0)) / M + 1e-06)
            weight_now = jnp.sqrt(weight_now * move_y / move_x)
        primal = primal_next
        dual = dual_next
    return (primal, dual)
```

```python
import functools

import jax
import jax.numpy as jnp
from jax import lax
from jax.experimental import pallas as pl
from jax.experimental.pallas import tpu as pltpu
from jax.sharding import PartitionSpec as P

ITERS = 3
STEP_SCALE = 0.5
LANES = 128
HALF = LANES // 2
TAIL = 16

bf16 = jnp.bfloat16
f32 = jnp.float32

SMEM = pl.BlockSpec(memory_space=pltpu.SMEM)
VMEM = pl.BlockSpec(memory_space=pltpu.VMEM)
ANY = pl.BlockSpec(memory_space=pl.ANY)


def swap_halves(values):
    return pltpu.roll(values, HALF, 1)


def low_lanes(shape):
    return lax.broadcasted_iota(jnp.int32, shape, 1) < HALF


def pack(upper, lower):
    return jnp.where(low_lanes(upper.shape), upper, swap_halves(lower))


def split_sum(total):
    first = total.astype(bf16).astype(f32)
    rest = total - first
    second = rest.astype(bf16).astype(f32)
    third = rest - second
    row = lax.broadcasted_iota(jnp.int32, (TAIL, LANES), 0)
    tile = jnp.where(row == 0, first, jnp.where(row == 1, second, jnp.where(row == 2, third, 0.0)))
    return tile.astype(bf16)


def join_sum(tile):
    return jnp.sum(tile.astype(f32), axis=0, keepdims=True)


def tree_sum(terms):
    terms = list(terms)
    while len(terms) > 1:
        terms = [terms[k] + terms[k + 1] for k in range(0, len(terms), 2)]
    return terms[0]


def column_total(squares):
    total = jnp.sum(squares, axis=0, keepdims=True)
    return total + swap_halves(jnp.broadcast_to(total, (8, LANES)))[0:1]


class Tiles:
    def __init__(self, tile_map, sources, slots, sems):
        self.tile_map, self.sources, self.slots, self.sems = tile_map, sources, slots, sems
        self.rows, self.cols = tile_map.shape
        self.size_r, self.size_c = slots.shape[1:]
        self.rows_each = self.rows // len(sources)

    def copy(self, source, i, j):
        spot = i * self.cols + j
        inner = i % self.rows_each
        return pltpu.make_async_copy(
            source.at[pl.ds(inner * self.size_r, self.size_r), pl.ds(j * self.size_c, self.size_c)],
            self.slots.at[spot],
            self.sems.at[spot],
        )

    def start(self):
        for i in range(self.rows):
            for j in range(self.cols):
                @pl.when(self.tile_map[i, j] != 0)
                def _():
                    self.copy(self.sources[i // self.rows_each], i, j).start()

    def each(self, body):
        def step(t, carry):
            i, j = t // self.cols, t % self.cols

            @pl.when(self.tile_map[i, j] != 0)
            def _():
                pltpu.make_async_copy(self.slots.at[t], self.slots.at[t], self.sems.at[t]).wait()
                body(i, j, self.slots[t])

            return carry

        lax.fori_loop(0, self.rows * self.cols, step, 0)


def product_back(tiles, vector, acc):
    acc[...] = jnp.zeros_like(acc)

    def body(i, j, tile):
        rows = vector[pl.ds(pl.multiple_of(i * tiles.size_r, tiles.size_r), tiles.size_r)]
        where = pl.ds(pl.multiple_of(j * tiles.size_c, tiles.size_c), tiles.size_c)
        acc[where] += lax.dot_general(
            tile, rows, (((0,), (0,)), ((), ())), preferred_element_type=f32
        )

    tiles.each(body)


def product_forward(tiles, vector, acc):
    acc[...] = jnp.zeros_like(acc)

    def body(i, j, tile):
        rows = vector[pl.ds(pl.multiple_of(j * tiles.size_c, tiles.size_c), tiles.size_c)]
        where = pl.ds(pl.multiple_of(i * tiles.size_r, tiles.size_r), tiles.size_r)
        acc[where] += jnp.dot(tile, rows, preferred_element_type=f32)

    tiles.each(body)


def first_kernel(tile_map, place, blocks, dual, mine, other, slots, sems, acc, vector):
    tiles = Tiles(tile_map, [blocks], slots, sems)
    tiles.start()
    vector[...] = dual[...].astype(bf16)
    product_back(tiles, vector, acc)

    @pl.when(place[1] == 0)
    def _():
        mine[...] = acc[:, :LANES]
        other[...] = acc[:, LANES:]

    @pl.when(place[1] != 0)
    def _():
        mine[...] = acc[:, LANES:]
        other[...] = acc[:, :LANES]


def first_pack_kernel(mine, other, msg_a, msg_b):
    half = msg_a.shape[0] - TAIL
    upper = mine[:half] + other[:half]
    lower = mine[half:] + other[half:]
    msg_a[:half] = pack(upper, lower).astype(bf16)
    msg_b[:half] = pack(swap_halves(upper), swap_halves(lower)).astype(bf16)
    msg_a[half:] = jnp.zeros((TAIL, LANES), bf16)
    msg_b[half:] = jnp.zeros((TAIL, LANES), bf16)


def back_kernel(count, tile_map, place, *refs):
    pieces = refs[:count]
    own, partner, msg, slots, sems, vector, acc = refs[count:]
    tiles = Tiles(tile_map, [own, partner], slots, sems)
    tiles.start()
    piece = pieces[0].shape[0] - TAIL
    half = vector.shape[0] // 2
    for k in range(count):
        start = pl.multiple_of((place[0] ^ k) * piece, piece)
        values = pieces[k][:piece]
        vector[pl.ds(start, piece)] = values
        vector[pl.ds(half + start, piece)] = swap_halves(values.astype(f32)).astype(bf16)
    product_back(tiles, vector, acc)
    out = msg.shape[0] - TAIL
    msg[:out] = pack(acc[:out], acc[out:]).astype(bf16)
    total = sum(join_sum(ref[piece:]) for ref in pieces)
    msg[out:] = split_sum(total)


def forward_kernel(
    near, count, first, last, total_rows, total_cols, tile_map, place, *refs
):
    msgs = refs[:near]
    primal, cost, lower, upper, state, own, partner = refs[near : near + 7]
    outs = refs[near + 7 :]
    primal_next, image_own = outs[:2]
    image_msgs = outs[2 : 1 + count]
    state_out, slots, sems, vector, acc = outs[1 + count :]
    tiles = Tiles(tile_map, [own, partner], slots, sems)
    tiles.start()
    size = primal.shape[0]
    weight = state[0:1]
    if not first:
        sum_y = tree_sum([join_sum(ref[size:]) for ref in msgs])
        move_y = jnp.sqrt(sum_y / total_rows + 1e-06)
        move_x = jnp.sqrt(state[1:2] / total_cols + 1e-06)
        weight = jnp.sqrt(weight * move_y / move_x)
    state_out[...] = jnp.broadcast_to(weight, state_out.shape)
    step = STEP_SCALE / weight
    image_t = tree_sum([ref[:size].astype(f32) for ref in msgs])
    before = primal[...]
    after = before - step * (cost[...] - image_t)
    after = jnp.minimum(jnp.maximum(after, lower[...]), upper[...])
    primal_next[...] = after
    extrapolated = 2.0 * after - before
    vector[:size] = extrapolated.astype(bf16)
    vector[size:] = swap_halves(extrapolated).astype(bf16)
    tail = None
    if not last:
        tail = split_sum(column_total((after - before) ** 2))
    product_forward(tiles, vector, acc)
    half = acc.shape[0] // 2
    piece = image_own.shape[0]
    for k in range(count):
        start = pl.multiple_of((place[0] ^ k) * piece, piece)
        part = pack(acc[pl.ds(start, piece)], acc[pl.ds(half + start, piece)])
        if k == 0:
            image_own[...] = part
        else:
            image_msgs[k - 1][:piece] = part.astype(bf16)
            image_msgs[k - 1][piece:] = jnp.zeros((TAIL, LANES), bf16) if last else tail
    if not last:
        state_out[1:2] = join_sum(tail)


def dual_kernel(count, last, *refs):
    image_own, state = refs[:2]
    msgs = refs[2 : 1 + count]
    dual, right, floor, dual_next = refs[1 + count : 5 + count]
    piece = image_own.shape[0]
    image = image_own[...]
    for ref in msgs:
        image = image + ref[:piece].astype(f32)
    before = dual[...]
    after = before + STEP_SCALE * state[0:1] * (right[...] - image)
    after = jnp.maximum(after, floor[...])
    dual_next[...] = after
    if not last:
        msg, state_out = refs[5 + count :]
        msg[:piece] = after.astype(bf16)
        msg[piece:] = split_sum(column_total((after - before) ** 2))
        sum_x = state[1:2]
        for ref in msgs:
            sum_x = sum_x + join_sum(ref[piece:])
        state_out[...] = state[...]
        state_out[1:2] = sum_x


def unpack_kernel(count, place, *refs):
    pieces_a, pieces_b = refs[:count], refs[count : 2 * count]
    upper, lower = refs[2 * count :]
    piece = pieces_a[0].shape[0]
    for k in range(count):
        start = pl.multiple_of((place[0] ^ k) * piece, piece) if count > 1 else 0
        a, b = pieces_a[k][...], pieces_b[k][...]
        low = low_lanes(a.shape)
        upper[pl.ds(start, piece)] = jnp.where(low, a, swap_halves(b))
        lower[pl.ds(start, piece)] = jnp.where(low, swap_halves(a), b)


def call(kernel, out_shape, in_specs, scratch=(), flops=0, name=None):
    return pl.pallas_call(
        kernel,
        out_shape=out_shape,
        in_specs=in_specs,
        out_specs=jax.tree.map(lambda _: VMEM, out_shape),
        scratch_shapes=list(scratch),
        compiler_params=pltpu.CompilerParams(vmem_limit_bytes=32 * 1024 * 1024),
        cost_estimate=pl.CostEstimate(flops=flops, bytes_accessed=4 << 20, transcendentals=0),
        name=name,
    )


def shape(rows, kind=f32, cols=LANES):
    return jax.ShapeDtypeStruct((rows, cols), kind)


def local(
    blocks,
    tile_map,
    lower_bound,
    upper_bound,
    bound_code,
    row_kind,
    cost_vector,
    right_side,
    primal_start,
    dual_start,
    primal_weight,
):
    rows, cols = blocks.shape
    size_r = rows // tile_map.shape[0]
    size_c = cols // tile_map.shape[1]
    count = lax.axis_size("col")
    near = lax.axis_size("row") // 2
    total_rows = rows * near * 2
    total_cols = cols * count
    piece = rows // count
    half = cols // 2
    z = lax.axis_index("col")
    core = lax.axis_index("row") % 2
    place = jnp.stack([z, core]).astype(jnp.int32)

    def to_core(value):
        return lax.ppermute(value, "row", [(i, i ^ 1) for i in range(2 * near)])

    def to_x(value, k):
        return lax.ppermute(value, "row", [(i, i ^ (2 * k)) for i in range(2 * near)])

    def to_z(value, k):
        return lax.ppermute(value, "col", [(i, i ^ k) for i in range(count)])

    def scratch(n_tiles):
        return [
            pltpu.VMEM((n_tiles, size_r, size_c), bf16),
            pltpu.SemaphoreType.DMA((n_tiles,)),
        ]

    n_own = tile_map.size

    with jax.named_scope("first_product"):
        mine, other = call(
            first_kernel,
            (shape(cols), shape(cols)),
            [SMEM, SMEM, ANY, VMEM],
            scratch(n_own) + [pltpu.VMEM((cols, 2 * LANES), f32), pltpu.VMEM((rows, 2 * LANES), bf16)],
            flops=2 * rows * cols * 256,
            name="first_product",
        )(tile_map, place, blocks, dual_start)
    other = to_core(other)
    messages = call(
        first_pack_kernel, (shape(half + TAIL, bf16),) * 2, [VMEM, VMEM], name="first_pack"
    )(mine, other)
    messages, blocks = lax.optimization_barrier((messages, blocks))
    partner = to_core(blocks)
    chip_map = jnp.concatenate([tile_map, to_core(tile_map)], axis=0)

    def my_half(value):
        return lax.dynamic_slice_in_dim(value, core * LANES, LANES, 1)

    def other_half(value):
        return lax.dynamic_slice_in_dim(value, (1 - core) * LANES, LANES, 1)

    def batches(upper, lower):
        return [
            jnp.concatenate([upper[:, b * HALF : (b + 1) * HALF], lower[:, b * HALF : (b + 1) * HALF]], axis=1)
            for b in range(2)
        ]

    def spread(vector):
        wide = jnp.broadcast_to(vector[:, None], (cols, HALF))
        return jnp.concatenate([wide[:half], wide[half:]], axis=1)

    start = my_half(primal_start)
    primal = batches(start[:half], start[half:])
    low_on = (bound_code == 1) | (bound_code == 3)
    high_on = (bound_code == 2) | (bound_code == 3)
    lower = spread(jnp.where(low_on, lower_bound, -jnp.inf))
    upper = spread(jnp.where(high_on, upper_bound, jnp.inf))
    cost = spread(cost_vector)

    def own_rows(value):
        return lax.dynamic_slice_in_dim(value, z * piece, piece, 0)

    floor = jnp.broadcast_to(jnp.where(own_rows(row_kind) == 1, 0.0, -jnp.inf)[:, None], (piece, LANES))
    dual_rows, right_rows = own_rows(dual_start), own_rows(right_side)
    received = to_core(jnp.concatenate([other_half(dual_rows), other_half(right_rows), floor], axis=0))
    dual = batches(my_half(dual_rows), received[:piece])
    right = batches(my_half(right_rows), received[piece : 2 * piece])
    floors = batches(floor, received[2 * piece :])

    weight = lax.dynamic_slice_in_dim(primal_weight, core * LANES, LANES, 0)
    state = [
        jnp.broadcast_to(jnp.tile(weight[b * HALF : (b + 1) * HALF], 2)[None, :], (8, LANES)) for b in range(2)
    ]

    n_chip = 2 * n_own
    flops = 2 * (2 * rows) * cols * LANES
    gathered = [None, None]
    for iteration in range(ITERS):
        first, last = iteration == 0, iteration + 1 == ITERS
        for b in range(2):
            if not first:
                messages = list(messages)
                messages[b] = call(
                    functools.partial(back_kernel, count),
                    shape(half + TAIL, bf16),
                    [SMEM, SMEM] + [VMEM] * count + [ANY, ANY],
                    scratch(n_chip) + [pltpu.VMEM((2 * rows, LANES), bf16), pltpu.VMEM((cols, LANES), f32)],
                    flops=flops,
                    name="back_product",
                )(chip_map, place, *gathered[b], blocks, partner)
            x_msgs = [messages[b]] + [to_x(messages[b], k) for k in range(1, near)]
            outs = call(
                functools.partial(forward_kernel, near, count, first, last, total_rows, total_cols),
                (shape(half), shape(piece)) + (shape(piece + TAIL, bf16),) * (count - 1) + (shape(8),),
                [SMEM, SMEM] + [VMEM] * (near + 5) + [ANY, ANY],
                scratch(n_chip) + [pltpu.VMEM((cols, LANES), bf16), pltpu.VMEM((2 * rows, LANES), f32)],
                flops=flops,
                name="forward_product",
            )(chip_map, place, *x_msgs, primal[b], cost, lower, upper, state[b], blocks, partner)
            primal[b], image_own, image_msgs, state_b = outs[0], outs[1], outs[2:-1], outs[-1]
            image_msgs = [to_z(image_msgs[k - 1], k) for k in range(1, count)]
            out_shape = (shape(piece),)
            if not last:
                out_shape += (shape(piece + TAIL, bf16), shape(8))
            outs = call(
                functools.partial(dual_kernel, count, last),
                out_shape,
                [VMEM] * (count + 4),
                name="dual_update",
            )(image_own, state_b, *image_msgs, dual[b], right[b], floors[b])
            dual[b] = outs[0]
            if last:
                gathered[b] = [dual[b]] + [to_z(dual[b], k) for k in range(1, count)]
            else:
                state[b] = outs[2]
                gathered[b] = [outs[1]] + [to_z(outs[1], k) for k in range(1, count)]

    def both(mine, theirs):
        return lax.cond(
            core == 0,
            lambda a, b: jnp.concatenate([a, b], axis=1),
            lambda a, b: jnp.concatenate([b, a], axis=1),
            mine,
            theirs,
        )

    upper, lower = call(
        functools.partial(unpack_kernel, 1), (shape(half), shape(half)), [SMEM, VMEM, VMEM], name="unpack_primal"
    )(place, *primal)
    primal_mine = jnp.concatenate([upper, lower], axis=0)
    primal_final = both(primal_mine, to_core(primal_mine))
    own, theirs = call(
        functools.partial(unpack_kernel, count),
        (shape(rows), shape(rows)),
        [SMEM] + [VMEM] * (2 * count),
        name="unpack_dual",
    )(place, *gathered[0], *gathered[1])
    dual_final = both(own, to_core(theirs))
    return primal_final, dual_final


def solution(mesh):
    return jax.shard_map(
        local,
        mesh=mesh,
        in_specs=(
            P("row", "col"),
            P("row", "col"),
            P("col"),
            P("col"),
            P("col"),
            P("row"),
            P("col"),
            P("row", "groups"),
            P("col", "groups"),
            P("row", "groups"),
            P("groups"),
        ),
        out_specs=(P("col", "groups"), P("row", "groups")),
        check_vma=False,
    )
```

```python
import functools

import jax
import jax.numpy as jnp
from jax import lax
from jax.experimental import pallas as pl
from jax.experimental.pallas import tpu as pltpu
from jax.sharding import PartitionSpec as P

ITERS = 3
STEP_SCALE = 0.5
BATCHES = 2
TAIL = 128

bf16 = jnp.bfloat16
f32 = jnp.float32

SMEM = pl.BlockSpec(memory_space=pltpu.SMEM)
VMEM = pl.BlockSpec(memory_space=pltpu.VMEM)
ANY = pl.BlockSpec(memory_space=pl.ANY)


def split_sum(total):
    first = total.astype(bf16).astype(f32)
    rest = total - first
    second = rest.astype(bf16).astype(f32)
    third = rest - second
    lane = lax.broadcasted_iota(jnp.int32, (total.shape[0], TAIL), 1)
    block = jnp.where(lane == 0, first, jnp.where(lane == 1, second, jnp.where(lane == 2, third, 0.0)))
    return block.astype(bf16)


def join_sum(block):
    return jnp.sum(block.astype(f32), axis=1, keepdims=True)


def tree_sum(terms):
    terms = list(terms)
    while len(terms) > 1:
        terms = [terms[k] + terms[k + 1] for k in range(0, len(terms), 2)]
    return terms[0]


def set_state(weight, total):
    lane = lax.broadcasted_iota(jnp.int32, (weight.shape[0], TAIL), 1)
    return jnp.where(lane == 0, weight, jnp.where(lane == 1, total, 0.0))


class Tiles:
    def __init__(self, tile_map, sources, slots, sems, order):
        self.tile_map, self.sources, self.slots, self.sems, self.order = tile_map, sources, slots, sems, order
        self.rows, self.cols = tile_map.shape
        self.size_r, self.size_c = slots.shape[1:]

    def start(self):
        each = self.rows // len(self.sources)
        self.n = jnp.int32(0)
        for i in range(self.rows):
            for j in range(self.cols):
                spot = i * self.cols + j
                nonzero = self.tile_map[i, j] != 0

                @pl.when(nonzero)
                def _():
                    pltpu.make_async_copy(
                        self.sources[i // each].at[
                            pl.ds(i % each * self.size_r, self.size_r), pl.ds(j * self.size_c, self.size_c)
                        ],
                        self.slots.at[spot],
                        self.sems.at[spot],
                    ).start()
                    self.order[self.n] = spot

                self.n = self.n + nonzero.astype(jnp.int32)

    def run(self, body):
        def several(first, width):
            spots = [self.order[first + q] for q in range(width)]
            for spot in spots:
                pltpu.make_async_copy(self.slots.at[spot], self.slots.at[spot], self.sems.at[spot]).wait()
            for spot in spots:
                body(spot // self.cols, spot % self.cols, self.slots[spot])

        def four(u, carry):
            several(u * 4, 4)
            return carry

        lax.fori_loop(0, self.n // 4, four, 0)
        pl.when(self.n % 4 >= 2)(lambda: several(self.n // 4 * 4, 2))
        pl.when(self.n % 2 == 1)(lambda: several(self.n - 1, 1))

    def back(self, vector, acc):
        acc[...] = jnp.zeros_like(acc)

        def body(i, j, tile):
            rows = vector[:, pl.ds(pl.multiple_of(i * self.size_r, self.size_r), self.size_r)]
            acc[:, pl.ds(pl.multiple_of(j * self.size_c, self.size_c), self.size_c)] += jnp.dot(
                rows, tile, preferred_element_type=f32
            )

        self.run(body)

    def forward(self, vector, acc):
        acc[...] = jnp.zeros_like(acc)

        def body(i, j, tile):
            cols = vector[:, pl.ds(pl.multiple_of(j * self.size_c, self.size_c), self.size_c)]
            acc[:, pl.ds(pl.multiple_of(i * self.size_r, self.size_r), self.size_r)] += lax.dot_general(
                cols, tile, (((1,), (1,)), ((), ())), preferred_element_type=f32
            )

        self.run(body)


def first_kernel(tile_map, place, blocks, dual, mine, other, slots, sems, order, vector, acc):
    tiles = Tiles(tile_map, [blocks], slots, sems, order)
    tiles.start()
    vector[...] = dual[...].T.astype(bf16)
    tiles.back(vector, acc)
    size = mine.shape[0]
    mine[...] = acc[pl.ds(pl.multiple_of(place[1] * size, size), size)]
    other[...] = acc[pl.ds(pl.multiple_of((1 - place[1]) * size, size), size)]


def first_pack_kernel(mine, other, *msgs):
    size, width = msgs[0].shape[0], mine.shape[1]
    for b, msg in enumerate(msgs):
        here = pl.ds(b * size, size)
        msg[:, :width] = (mine[here] + other[here]).astype(bf16)
        msg[:, width:] = jnp.zeros((size, TAIL), bf16)


def back_kernel(tile_map, place, own_half, got_half, own, partner, msg, slots, sems, order, vector, acc):
    tiles = Tiles(tile_map, [own, partner], slots, sems, order)
    tiles.start()
    half = vector.shape[1] // 2
    side = place[0] % 2
    vector[:, pl.ds(pl.multiple_of(side * half, half), half)] = own_half[:, :half]
    vector[:, pl.ds(pl.multiple_of((1 - side) * half, half), half)] = got_half[:, :half]
    tiles.back(vector, acc)
    width = acc.shape[1]
    msg[:, :width] = acc[...].astype(bf16)
    msg[:, width:] = split_sum(join_sum(own_half[:, half:]) + join_sum(got_half[:, half:]))


def forward_kernel(near, first, last, total_rows, total_cols, tile_map, place, *refs):
    msgs = refs[:near]
    primal, vectors, state, own, partner = refs[near : near + 5]
    primal_next, kept, sent, state_out, slots, sems, order, vector, acc = refs[near + 5 :]
    tiles = Tiles(tile_map, [own, partner], slots, sems, order)
    tiles.start()
    width = primal.shape[1]
    weight = state[:, 0:1]
    if not first:
        sum_y = tree_sum([join_sum(ref[:, width:]) for ref in msgs])
        move_y = jnp.sqrt(sum_y / total_rows + 1e-06)
        move_x = jnp.sqrt(state[:, 1:2] / total_cols + 1e-06)
        weight = jnp.sqrt(weight * move_y / move_x)
    step = STEP_SCALE / weight
    image_t = tree_sum([ref[:, :width].astype(f32) for ref in msgs])
    before = primal[...]
    after = before - step * (vectors[0:1] - image_t)
    after = jnp.minimum(jnp.maximum(after, vectors[1:2]), vectors[2:3])
    primal_next[...] = after
    vector[...] = (2.0 * after - before).astype(bf16)
    sum_x = jnp.zeros_like(weight) if last else jnp.sum((after - before) ** 2, axis=1, keepdims=True)
    state_out[...] = set_state(weight, sum_x)
    tiles.forward(vector, acc)
    half = acc.shape[1] // 2
    side = place[0] % 2
    kept[...] = acc[:, pl.ds(pl.multiple_of(side * half, half), half)]
    sent[:, :half] = acc[:, pl.ds(pl.multiple_of((1 - side) * half, half), half)].astype(bf16)
    sent[:, half:] = split_sum(sum_x)


def pair_kernel(kept, state, got, msg):
    half = kept.shape[1]
    msg[:, :half] = (kept[...] + got[:, :half].astype(f32)).astype(bf16)
    msg[:, half:] = split_sum(state[:, 1:2] + join_sum(got[:, half:]))


def cross_kernel(own, got, msg):
    half = own.shape[1] - TAIL
    msg[:, :half] = (own[:, :half].astype(f32) + got[:, :half].astype(f32)).astype(bf16)
    msg[:, half:] = split_sum(join_sum(own[:, half:]) + join_sum(got[:, half:]))


def dual_kernel(last, own, got, state, dual, right, floor, dual_next, *outs):
    half = dual.shape[1]
    image = own[:, :half].astype(f32) + got[:, :half].astype(f32)
    before = dual[...]
    weight = state[:, 0:1]
    after = before + STEP_SCALE * weight * (right[...] - image)
    after = jnp.maximum(after, floor[0:1])
    dual_next[...] = after
    if not last:
        msg, state_out = outs
        msg[:, :half] = after.astype(bf16)
        msg[:, half:] = split_sum(jnp.sum((after - before) ** 2, axis=1, keepdims=True))
        state_out[...] = set_state(weight, join_sum(own[:, half:]) + join_sum(got[:, half:]))


def turn_kernel(place, value, *outs):
    size = outs[0].shape[0]
    width = size * len(outs)
    turned = value[:, pl.ds(pl.multiple_of(place[1] * width, width), width)].T
    for b, out in enumerate(outs):
        out[...] = turned[b * size : (b + 1) * size]


def rows_kernel(place, dual, right, got, *outs):
    size = outs[0].shape[0]
    width = size * BATCHES
    rows = dual.shape[0]
    here = pl.ds(pl.multiple_of(place[1] * width, width), width)

    def put(values, outs):
        turned = values.T
        for b, out in enumerate(outs):
            out[...] = turned[b * size : (b + 1) * size]

    @pl.when(place[0] % 2 == 0)
    def _():
        put(dual[:, here], outs[:BATCHES])
        put(right[:, here], outs[BATCHES:])

    @pl.when(place[0] % 2 == 1)
    def _():
        put(got[:rows], outs[:BATCHES])
        put(got[rows:], outs[BATCHES:])


def primal_out_kernel(place, *refs):
    mine, theirs, out = refs[:BATCHES], refs[BATCHES:-1], refs[-1]
    width = out.shape[1] // 2
    out[:, pl.ds(pl.multiple_of(place[1] * width, width), width)] = jnp.concatenate([r[...] for r in mine], axis=0).T
    out[:, pl.ds(pl.multiple_of((1 - place[1]) * width, width), width)] = jnp.concatenate(
        [r[...] for r in theirs], axis=0
    ).T


def choose_kernel(place, own, got, mine, other):
    @pl.when(place[0] % 2 == 0)
    def _():
        mine[...] = own[...]
        other[...] = got[...]

    @pl.when(place[0] % 2 == 1)
    def _():
        mine[...] = got[...]
        other[...] = own[...]


def call(kernel, out_shape, in_specs, scratch=(), flops=0, name=None):
    return pl.pallas_call(
        kernel,
        out_shape=out_shape,
        in_specs=in_specs,
        out_specs=jax.tree.map(lambda _: VMEM, out_shape),
        scratch_shapes=list(scratch),
        compiler_params=pltpu.CompilerParams(vmem_limit_bytes=32 * 1024 * 1024),
        cost_estimate=pl.CostEstimate(flops=flops, bytes_accessed=4 << 20, transcendentals=0),
        name=name,
    )


def shape(rows, cols, kind=f32):
    return jax.ShapeDtypeStruct((rows, cols), kind)


def local(
    blocks,
    tile_map,
    lower_bound,
    upper_bound,
    bound_code,
    row_kind,
    cost_vector,
    right_side,
    primal_start,
    dual_start,
    primal_weight,
):
    rows, cols = blocks.shape
    size_r = rows // tile_map.shape[0]
    size_c = cols // tile_map.shape[1]
    profiles = dual_start.shape[1]
    width = profiles // 2
    size = width // BATCHES
    count = lax.axis_size("col")
    near = lax.axis_size("row") // 2
    total_rows = rows * near * 2
    total_cols = cols * count
    z = lax.axis_index("col")
    core = lax.axis_index("row") % 2
    place = jnp.stack([z, core]).astype(jnp.int32)

    def to_core(value):
        return lax.ppermute(value, "row", [(i, i ^ 1) for i in range(2 * near)])

    def to_x(value, k):
        return lax.ppermute(value, "row", [(i, i ^ (2 * k)) for i in range(2 * near)])

    def to_z(value, k):
        return lax.ppermute(value, "col", [(i, i ^ k) for i in range(count)])

    def scratch(n_tiles, batch, depth, out):
        return [
            pltpu.VMEM((n_tiles, size_r, size_c), bf16),
            pltpu.SemaphoreType.DMA((n_tiles,)),
            pltpu.SMEM((n_tiles,), jnp.int32),
            pltpu.VMEM((batch, depth), bf16),
            pltpu.VMEM((batch, out), f32),
        ]

    n_own = tile_map.size
    n_chip = 2 * n_own

    with jax.named_scope("first_product"):
        mine, other = call(
            first_kernel,
            (shape(width, cols),) * 2,
            [SMEM, SMEM, ANY, VMEM],
            scratch(n_own, profiles, rows, cols),
            flops=2 * rows * cols * profiles,
            name="first_product",
        )(tile_map, place, blocks, dual_start)
    other = to_core(other)
    messages = list(
        call(first_pack_kernel, (shape(size, cols + TAIL, bf16),) * BATCHES, [VMEM] * 2, name="first_pack")(
            mine, other
        )
    )
    partner = to_core(blocks)
    chip_map = jnp.concatenate([tile_map, to_core(tile_map)], axis=0)

    primal = list(call(turn_kernel, (shape(size, cols),) * BATCHES, [SMEM, VMEM], name="turn_primal")(place, primal_start))
    low_on = (bound_code == 1) | (bound_code == 3)
    high_on = (bound_code == 2) | (bound_code == 3)
    vectors = jnp.stack(
        [cost_vector, jnp.where(low_on, lower_bound, -jnp.inf), jnp.where(high_on, upper_bound, jnp.inf)]
    )

    def other_half(value):
        return lax.dynamic_slice_in_dim(value, (1 - core) * width, width, 1)

    received = to_core(jnp.concatenate([other_half(dual_start), other_half(right_side)], axis=0))
    kind = jnp.where(z % 2 == 0, row_kind, to_core(row_kind))
    floor = jnp.where(kind == 1, 0.0, -jnp.inf).astype(f32)[None, :]
    held = call(
        rows_kernel, (shape(size, rows),) * (2 * BATCHES), [SMEM] + [VMEM] * 3, name="turn_rows"
    )(place, dual_start, right_side, received)
    dual, right = list(held[:BATCHES]), held[BATCHES:]

    weight = lax.dynamic_slice_in_dim(primal_weight, core * width, width, 0)
    state = [jnp.broadcast_to(weight[b * size : (b + 1) * size, None], (size, TAIL)) for b in range(BATCHES)]

    flops = 2 * (2 * rows) * cols * size
    half_msg = shape(size, rows + TAIL, bf16)
    halves = [None] * BATCHES
    for iteration in range(ITERS):
        first, last = iteration == 0, iteration + 1 == ITERS
        for b in range(BATCHES):
            if not first:
                messages[b] = call(
                    back_kernel,
                    shape(size, cols + TAIL, bf16),
                    [SMEM, SMEM, VMEM, VMEM, ANY, ANY],
                    scratch(n_chip, size, 2 * rows, cols),
                    flops=flops,
                    name="back_product",
                )(chip_map, place, *halves[b], blocks, partner)
            x_msgs = [messages[b]] + [to_x(messages[b], k) for k in range(1, near)]
            primal[b], kept, sent, state[b] = call(
                functools.partial(forward_kernel, near, first, last, total_rows, total_cols),
                (shape(size, cols), shape(size, rows), half_msg, shape(size, TAIL)),
                [SMEM, SMEM] + [VMEM] * (near + 3) + [ANY, ANY],
                scratch(n_chip, size, cols, 2 * rows),
                flops=flops,
                name="forward_product",
            )(chip_map, place, *x_msgs, primal[b], vectors, state[b], blocks, partner)
            own = call(pair_kernel, half_msg, [VMEM] * 3, name="pair_sum")(kept, state[b], to_z(sent, 1))
            mask = 2
            while mask * 2 < count:
                own = call(cross_kernel, half_msg, [VMEM] * 2, name="cross_sum")(own, to_z(own, mask))
                mask *= 2
            got = to_z(own, mask)
            out_shape = (shape(size, rows),)
            if not last:
                out_shape += (half_msg, shape(size, TAIL))
            outs = call(functools.partial(dual_kernel, last), out_shape, [VMEM] * 6, name="dual_update")(
                own, got, state[b], dual[b], right[b], floor
            )
            dual[b] = outs[0]
            if not last:
                state[b] = outs[2]
                halves[b] = (outs[1], to_z(outs[1], 1))

    primal_final = call(
        primal_out_kernel, shape(cols, profiles), [SMEM] + [VMEM] * (2 * BATCHES), name="primal_out"
    )(place, *primal, *[to_core(p) for p in primal])
    mine, theirs = [], []
    for b in range(BATCHES):
        own, other = call(choose_kernel, (shape(size, rows),) * 2, [SMEM, VMEM, VMEM], name="choose_rows")(
            place, dual[b], to_z(dual[b], 1)
        )
        mine.append(own)
        theirs.append(to_core(other))
    dual_final = call(
        primal_out_kernel, shape(rows, profiles), [SMEM] + [VMEM] * (2 * BATCHES), name="dual_out"
    )(place, *mine, *theirs)
    return primal_final, dual_final


def solution(mesh):
    return jax.shard_map(
        local,
        mesh=mesh,
        in_specs=(
            P("row", "col"),
            P("row", "col"),
            P("col"),
            P("col"),
            P("col"),
            P("row"),
            P("col"),
            P("row", "groups"),
            P("col", "groups"),
            P("row", "groups"),
            P("groups"),
        ),
        out_specs=(P("col", "groups"), P("row", "groups")),
        check_vma=False,
    )
```

```python
import functools

import jax
import jax.numpy as jnp
from jax import lax
from jax.experimental import pallas as pl
from jax.experimental.pallas import tpu as pltpu
from jax.sharding import PartitionSpec as P

ITERS = 3
STEP_SCALE = 0.5
BATCHES = 2
TAIL = 128

bf16 = jnp.bfloat16
f32 = jnp.float32

SMEM = pl.BlockSpec(memory_space=pltpu.SMEM)
VMEM = pl.BlockSpec(memory_space=pltpu.VMEM)
ANY = pl.BlockSpec(memory_space=pl.ANY)
HBM = pl.BlockSpec(memory_space=pltpu.HBM)


def split_sum(total):
    first = total.astype(bf16).astype(f32)
    rest = total - first
    second = rest.astype(bf16).astype(f32)
    third = rest - second
    lane = lax.broadcasted_iota(jnp.int32, (total.shape[0], TAIL), 1)
    block = jnp.where(lane == 0, first, jnp.where(lane == 1, second, jnp.where(lane == 2, third, 0.0)))
    return block.astype(bf16)


def join_sum(block):
    return jnp.sum(block.astype(f32), axis=1, keepdims=True)


def tree_sum(terms):
    terms = list(terms)
    while len(terms) > 1:
        terms = [terms[k] + terms[k + 1] for k in range(0, len(terms), 2)]
    return terms[0]


def set_state(weight, total):
    lane = lax.broadcasted_iota(jnp.int32, (weight.shape[0], TAIL), 1)
    return jnp.where(lane == 0, weight, jnp.where(lane == 1, total, 0.0))


class Blocks:
    def __init__(self, order, slots, cols):
        self.order, self.slots, self.cols = order, slots, cols
        self.n = order[order.shape[0] - 1]

    def ready(self, spot):
        pass

    def run(self, body):
        def several(first, width):
            spots = [self.order[first + q] for q in range(width)]
            for spot in spots:
                self.ready(spot)
            for spot in spots:
                body(spot // self.cols, spot % self.cols, self.slots[spot])

        def four(u, carry):
            several(u * 4, 4)
            return carry

        lax.fori_loop(0, self.n // 4, four, 0)
        pl.when(self.n % 4 >= 2)(lambda: several(self.n // 4 * 4, 2))
        pl.when(self.n % 2 == 1)(lambda: several(self.n - 1, 1))

    def back(self, vector, acc):
        size_r, size_c = self.slots.shape[1:]
        acc[...] = jnp.zeros_like(acc)

        def body(i, j, block):
            rows = vector[:, pl.ds(pl.multiple_of(i * size_r, size_r), size_r)]
            acc[:, pl.ds(pl.multiple_of(j * size_c, size_c), size_c)] += jnp.dot(
                rows, block, preferred_element_type=f32
            )

        self.run(body)

    def forward(self, vector, acc):
        size_c, size_r = self.slots.shape[1:]
        acc[...] = jnp.zeros_like(acc)

        def body(i, j, block):
            cols = vector[:, pl.ds(pl.multiple_of(j * size_c, size_c), size_c)]
            acc[:, pl.ds(pl.multiple_of(i * size_r, size_r), size_r)] += jnp.dot(
                cols, block, preferred_element_type=f32
            )

        self.run(body)


class Incoming(Blocks):
    def __init__(self, tile_map, sources, slots, sems, order):
        rows, cols = tile_map.shape
        size_r, size_c = slots.shape[1:]
        each = rows // len(sources)
        n = jnp.int32(0)
        for i in range(rows):
            for j in range(cols):
                spot = i * cols + j
                nonzero = tile_map[i, j] != 0

                @pl.when(nonzero)
                def _():
                    pltpu.make_async_copy(
                        sources[i // each].at[pl.ds(i % each * size_r, size_r), pl.ds(j * size_c, size_c)],
                        slots.at[spot],
                        sems.at[spot],
                    ).start()
                    order[n] = spot

                n = n + nonzero.astype(jnp.int32)
        order[order.shape[0] - 1] = n
        self.sems = sems
        super().__init__(order, slots, cols)
        self.n = n

    def ready(self, spot):
        pltpu.make_async_copy(self.slots.at[spot], self.slots.at[spot], self.sems.at[spot]).wait()


def first_kernel(tile_map, place, blocks, dual, mine, other, slots, sems, order, vector, acc):
    incoming = Incoming(tile_map, [blocks], slots, sems, order)
    vector[...] = dual[...].T.astype(bf16)
    incoming.back(vector, acc)
    size = mine.shape[0]
    mine[...] = acc[pl.ds(pl.multiple_of(place[1] * size, size), size)]
    other[...] = acc[pl.ds(pl.multiple_of((1 - place[1]) * size, size), size)]


def load_kernel(tile_map, own, partner, *refs):
    slots, turned, order, sems = refs[-4:]
    incoming = Incoming(tile_map, [own, partner], slots, sems, order)

    def one(q, carry):
        spot = order[q]
        incoming.ready(spot)
        turned[spot] = slots[spot].T
        return carry

    lax.fori_loop(0, incoming.n, one, 0)


def first_pack_kernel(batch, mine, other, after, msg):
    size = msg.shape[0]
    here = pl.ds(batch * size, size)
    msg[...] = (mine[here] + other[here]).astype(bf16)


def back_kernel(grid_cols, order, place, own_half, got_half, slots, after, msg, vector, acc):
    half = vector.shape[1] // 2
    side = place[0] % 2
    vector[:, pl.ds(pl.multiple_of(side * half, half), half)] = own_half[:, :half]
    vector[:, pl.ds(pl.multiple_of((1 - side) * half, half), half)] = got_half[:, :half]
    Blocks(order, slots, grid_cols).back(vector, acc)
    width = acc.shape[1]
    msg[:, :width] = acc[...].astype(bf16)
    msg[:, width:] = split_sum(join_sum(own_half[:, half:]) + join_sum(got_half[:, half:]))


def forward_kernel(grid_cols, near, first, last, total_rows, total_cols, order, place, *refs):
    msgs = refs[:near]
    primal, vectors, state, turned, after_ref = refs[near : near + 5]
    primal_next, kept, sent, state_out, vector, acc = refs[near + 5 :]
    width = primal.shape[1]
    weight = state[:, 0:1]
    if not first:
        sum_y = tree_sum([join_sum(ref[:, width:]) for ref in msgs])
        move_y = jnp.sqrt(sum_y / total_rows + 1e-06)
        move_x = jnp.sqrt(state[:, 1:2] / total_cols + 1e-06)
        weight = jnp.sqrt(weight * move_y / move_x)
    step = STEP_SCALE / weight
    image_t = tree_sum([ref[:, :width].astype(f32) for ref in msgs])
    before = primal[...]
    after = before - step * (vectors[0:1] - image_t)
    after = jnp.minimum(jnp.maximum(after, vectors[1:2]), vectors[2:3])
    primal_next[...] = after
    vector[...] = (2.0 * after - before).astype(bf16)
    sum_x = jnp.zeros_like(weight) if last else jnp.sum((after - before) ** 2, axis=1, keepdims=True)
    state_out[...] = set_state(weight, sum_x)
    if not last:
        sent[:, sent.shape[1] - TAIL :] = split_sum(sum_x)
    Blocks(order, turned, grid_cols).forward(vector, acc)
    half = acc.shape[1] // 2
    side = place[0] % 2
    kept[...] = acc[:, pl.ds(pl.multiple_of(side * half, half), half)]
    sent[:, :half] = acc[:, pl.ds(pl.multiple_of((1 - side) * half, half), half)].astype(bf16)


def pair_kernel(kept, state, got, after, msg):
    half = kept.shape[1]
    msg[:, :half] = (kept[...] + got[:, :half].astype(f32)).astype(bf16)
    if msg.shape[1] > half:
        msg[:, half:] = split_sum(state[:, 1:2] + join_sum(got[:, half:]))


def cross_kernel(half, own, got, msg):
    msg[:, :half] = (own[:, :half].astype(f32) + got[:, :half].astype(f32)).astype(bf16)
    if msg.shape[1] > half:
        msg[:, half:] = split_sum(join_sum(own[:, half:]) + join_sum(got[:, half:]))


def dual_kernel(last, own, got, state, dual, right, floor, after_ref, dual_next, *outs):
    half = dual.shape[1]
    image = own[:, :half].astype(f32) + got[:, :half].astype(f32)
    before = dual[...]
    weight = state[:, 0:1]
    after = before + STEP_SCALE * weight * (right[...] - image)
    after = jnp.maximum(after, floor[0:1])
    dual_next[...] = after
    if not last:
        msg, state_out = outs
        msg[:, :half] = after.astype(bf16)
        msg[:, half:] = split_sum(jnp.sum((after - before) ** 2, axis=1, keepdims=True))
        state_out[...] = set_state(weight, join_sum(own[:, half:]) + join_sum(got[:, half:]))


def turn_kernel(place, value, after, *outs):
    size = outs[0].shape[0]
    width = size * len(outs)
    turned = value[:, pl.ds(pl.multiple_of(place[1] * width, width), width)].T
    for b, out in enumerate(outs):
        out[...] = turned[b * size : (b + 1) * size]


def halves_kernel(place, dual, right, after, out):
    rows, width = dual.shape[0], out.shape[1]
    there = pl.ds(pl.multiple_of((1 - place[1]) * width, width), width)
    out[:rows] = dual[:, there]
    out[rows:] = right[:, there]


def rows_kernel(place, dual, right, got, after, *outs):
    size = outs[0].shape[0]
    width = size * BATCHES
    rows = dual.shape[0]
    here = pl.ds(pl.multiple_of(place[1] * width, width), width)

    def put(values, outs):
        turned = values.T
        for b, out in enumerate(outs):
            out[...] = turned[b * size : (b + 1) * size]

    @pl.when(place[0] % 2 == 0)
    def _():
        put(dual[:, here], outs[:BATCHES])
        put(right[:, here], outs[BATCHES:])

    @pl.when(place[0] % 2 == 1)
    def _():
        put(got[:rows], outs[:BATCHES])
        put(got[rows:], outs[BATCHES:])


def put_half(out, core, parts):
    width = out.shape[1] // 2
    out[:, pl.ds(pl.multiple_of(core * width, width), width)] = jnp.concatenate([r[...] for r in parts], axis=0).T


def primal_out_kernel(place, *refs):
    mine, theirs, out = refs[:BATCHES], refs[BATCHES : 2 * BATCHES], refs[-1]
    put_half(out, place[1], mine)
    put_half(out, 1 - place[1], theirs)


def dual_out_kernel(place, *refs):
    own, got, partner = refs[:BATCHES], refs[BATCHES : 2 * BATCHES], refs[2 * BATCHES : 3 * BATCHES]
    out = refs[-1]

    @pl.when(place[0] % 2 == 0)
    def _():
        put_half(out, place[1], own)
        put_half(out, 1 - place[1], got)

    @pl.when(place[0] % 2 == 1)
    def _():
        put_half(out, place[1], got)
        put_half(out, 1 - place[1], partner)


def call(kernel, out_shape, in_specs, scratch=(), name=None, vmem=6, out_specs=None):
    return pl.pallas_call(
        kernel,
        out_shape=out_shape,
        in_specs=in_specs,
        out_specs=out_specs or jax.tree.map(lambda _: VMEM, out_shape),
        scratch_shapes=list(scratch),
        compiler_params=pltpu.CompilerParams(vmem_limit_bytes=vmem << 20),
        cost_estimate=pl.CostEstimate(flops=0, bytes_accessed=0, transcendentals=0),
        name=name,
    )


def shape(rows, cols, kind=f32):
    return jax.ShapeDtypeStruct((rows, cols), kind)


def local(
    blocks,
    tile_map,
    lower_bound,
    upper_bound,
    bound_code,
    row_kind,
    cost_vector,
    right_side,
    primal_start,
    dual_start,
    primal_weight,
):
    rows, cols = blocks.shape
    size_r = rows // tile_map.shape[0]
    size_c = cols // tile_map.shape[1]
    profiles = dual_start.shape[1]
    width = profiles // 2
    size = width // BATCHES
    count = lax.axis_size("col")
    near = lax.axis_size("row") // 2
    total_rows = rows * near * 2
    total_cols = cols * count
    z = lax.axis_index("col")
    core = lax.axis_index("row") % 2
    place = jnp.stack([z, core]).astype(jnp.int32)

    def to_core(value):
        return lax.ppermute(value, "row", [(i, i ^ 1) for i in range(2 * near)])

    def to_x(value, k):
        return lax.ppermute(value, "row", [(i, i ^ (2 * k)) for i in range(2 * near)])

    def to_z(value, k):
        return lax.ppermute(value, "col", [(i, i ^ k) for i in range(count)])

    n_own = tile_map.size
    n_chip = 2 * n_own
    grid_cols = tile_map.shape[1]

    blocks = pltpu.with_memory_space_constraint(blocks, pltpu.HBM)
    partner = to_core(blocks)
    chip_map = jnp.concatenate([tile_map, to_core(tile_map)], axis=0)
    mine, other = call(
        first_kernel,
        (shape(width, cols),) * 2,
        [SMEM, SMEM, HBM, VMEM],
        [
            pltpu.VMEM((n_own, size_r, size_c), bf16),
            pltpu.SemaphoreType.DMA((n_own,)),
            pltpu.SMEM((n_own + 1,), jnp.int32),
            pltpu.VMEM((profiles, rows), bf16),
            pltpu.VMEM((profiles, cols), f32),
        ],
        name="first_product",
        vmem=16,
    )(tile_map, place, blocks, dual_start)
    other = to_core(other)

    low_on = (bound_code == 1) | (bound_code == 3)
    high_on = (bound_code == 2) | (bound_code == 3)
    vectors = jnp.stack(
        [cost_vector, jnp.where(low_on, lower_bound, -jnp.inf), jnp.where(high_on, upper_bound, jnp.inf)]
    )
    weight = lax.dynamic_slice_in_dim(primal_weight, core * width, width, 0)
    state = [jnp.broadcast_to(weight[b * size : (b + 1) * size, None], (size, TAIL)) for b in range(BATCHES)]
    kind = jnp.where(z % 2 == 0, row_kind, to_core(row_kind))
    floor = jnp.where(kind == 1, 0.0, -jnp.inf).astype(f32)[None, :]

    def half_msg(tail):
        return shape(size, rows + (TAIL if tail else 0), bf16)

    def back(b, iteration, after):
        if iteration == 0:
            messages[b] = call(
                functools.partial(first_pack_kernel, b),
                shape(size, cols, bf16),
                [VMEM] * 2 + [ANY],
                name="first_pack",
            )(mine, other, after)
        else:
            messages[b] = call(
                functools.partial(back_kernel, grid_cols),
                shape(size, cols + TAIL, bf16),
                [SMEM, SMEM, VMEM, VMEM, VMEM, ANY],
                [pltpu.VMEM((size, 2 * rows), bf16), pltpu.VMEM((size, cols), f32)],
                name="back_product",
            )(order, place, *halves[b], slots, after)
        return messages[b]

    def forward(b, iteration, after):
        first, last = iteration == 0, iteration + 1 == ITERS
        msgs = [messages[b]] + [to_x(messages[b], k) for k in range(1, near)]
        outs = call(
            functools.partial(forward_kernel, grid_cols, near, first, last, total_rows, total_cols),
            (shape(size, cols), shape(size, rows), half_msg(not last), shape(size, TAIL)),
            [SMEM, SMEM] + [VMEM] * (near + 4) + [ANY],
            [pltpu.VMEM((size, cols), bf16), pltpu.VMEM((size, 2 * rows), f32)],
            name="forward_product",
        )(order, place, *msgs, primal[b], vectors, state[b], turned, after)
        primal[b], kept[b], sent[b], state[b] = outs
        return state[b]

    def pair(b, iteration, after):
        out = half_msg(iteration + 1 < ITERS)
        crossing[b] = call(pair_kernel, out, [VMEM] * 3 + [ANY], name="pair_sum")(
            kept[b], state[b], to_z(sent[b], 1), after
        )
        mask = 2
        while mask * 2 < count:
            crossing[b] = call(functools.partial(cross_kernel, rows), out, [VMEM] * 2, name="cross_sum")(
                crossing[b], to_z(crossing[b], mask)
            )
            mask *= 2
        return crossing[b]

    def update(b, iteration, after):
        last = iteration + 1 == ITERS
        got = to_z(crossing[b], count // 2)
        out_shape = (shape(size, rows),)
        if not last:
            out_shape += (half_msg(True), shape(size, TAIL))
        outs = call(functools.partial(dual_kernel, last), out_shape, [VMEM] * 6 + [ANY], name="dual_update")(
            crossing[b], got, state[b], dual[b], right[b], floor, after
        )
        dual[b] = outs[0]
        if last:
            return dual[b]
        state[b] = outs[2]
        halves[b] = (outs[1], to_z(outs[1], 1))
        return state[b]

    stages = [(stage, k) for k in range(ITERS) for stage in (back, forward, pair, update)]
    lag = 4 // BATCHES
    messages, halves, kept, sent, crossing = ([None] * BATCHES for _ in range(5))
    token = state[0]
    primal_final = None
    for slot in range(len(stages) + lag * (BATCHES - 1)):
        for b in range(BATCHES):
            at = slot - lag * b
            if not 0 <= at < len(stages):
                continue
            stage, iteration = stages[at]
            token = stage(b, iteration, token)
            if (b, at) == (0, 0):
                primal = list(
                    call(turn_kernel, (shape(size, cols),) * BATCHES, [SMEM, VMEM, ANY], name="turn_primal")(
                        place, primal_start, token
                    )
                )
                spare = call(halves_kernel, shape(2 * rows, width), [SMEM, VMEM, VMEM, ANY], name="partner_half")(
                    place, dual_start, right_side, token
                )
                spare = to_core(spare)
                slots, turned, order = call(
                    load_kernel,
                    (
                        pltpu.VMEM((n_chip, size_r, size_c), bf16),
                        pltpu.VMEM((n_chip, size_c, size_r), bf16),
                        jax.ShapeDtypeStruct((n_chip + 1,), jnp.int32),
                    ),
                    [SMEM, HBM, HBM] + [ANY] * (3 + BATCHES),
                    [pltpu.SemaphoreType.DMA((n_chip,))],
                    name="load_blocks",
                    vmem=4,
                    out_specs=(VMEM, VMEM, SMEM),
                )(chip_map, blocks, partner, token, floor, vectors, *state)
            if (b, at) == (0, 1):
                held = call(
                    rows_kernel,
                    (shape(size, rows),) * (2 * BATCHES),
                    [SMEM] + [VMEM] * 3 + [ANY],
                    name="turn_rows",
                )(place, dual_start, right_side, spare, token)
                dual, right = list(held[:BATCHES]), held[BATCHES:]
            if (b, at) == (BATCHES - 1, len(stages) - 2):
                token = primal_final = call(
                    primal_out_kernel,
                    shape(cols, profiles),
                    [SMEM] + [VMEM] * (2 * BATCHES) + [ANY],
                    name="primal_out",
                )(place, *primal, *[to_core(p) for p in primal], token)

    def index(row, col):
        return row * count + col

    everyone = [(row, col) for row in range(2 * near) for col in range(count)]
    to_holder = [(index(r, c), index(r ^ (c % 2), c ^ 1)) for r, c in everyone]
    to_odd = [(index(r, c), index(r ^ 1, c)) for r, c in everyone if c % 2]
    got = [lax.ppermute(d, ("row", "col"), to_holder) for d in dual]
    partner_rows = [lax.ppermute(d, ("row", "col"), to_odd) for d in dual]
    dual_final = call(
        dual_out_kernel, shape(rows, profiles), [SMEM] + [VMEM] * (3 * BATCHES), name="dual_out"
    )(place, *dual, *got, *partner_rows)
    return primal_final, dual_final


def solution(mesh):
    return jax.shard_map(
        local,
        mesh=mesh,
        in_specs=(
            P("row", "col"),
            P("row", "col"),
            P("col"),
            P("col"),
            P("col"),
            P("row"),
            P("col"),
            P("row", "groups"),
            P("col", "groups"),
            P("row", "groups"),
            P("groups"),
        ),
        out_specs=(P("col", "groups"), P("row", "groups")),
        check_vma=False,
    )
```

```python
import functools

import jax
import jax.numpy as jnp
from jax import lax
from jax.experimental import pallas as pl
from jax.experimental.pallas import tpu as pltpu
from jax.sharding import PartitionSpec as P

ITERS = 3
STEP_SCALE = 0.5
BATCHES = 2
LAG = 1
STAGE_FLOPS = 4 * 10**9
TAIL = 128

bf16 = jnp.bfloat16
f32 = jnp.float32

SMEM = pl.BlockSpec(memory_space=pltpu.SMEM)
VMEM = pl.BlockSpec(memory_space=pltpu.VMEM)
ANY = pl.BlockSpec(memory_space=pl.ANY)
HBM = pl.BlockSpec(memory_space=pltpu.HBM)


def split_sums(*totals):
    lane = lax.broadcasted_iota(jnp.int32, (totals[0].shape[0], TAIL), 1)
    block = jnp.zeros(lane.shape, f32)
    for k, rest in enumerate(totals):
        for part in range(3):
            rounded = rest.astype(bf16).astype(f32)
            block = jnp.where(lane == 3 * k + part, rounded, block)
            rest = rest - rounded
    return block.astype(bf16)


def join_sum(block, k=0):
    lane = lax.broadcasted_iota(jnp.int32, block.shape, 1)
    mine = (lane >= 3 * k) & (lane < 3 * k + 3)
    return jnp.sum(jnp.where(mine, block.astype(f32), 0.0), axis=1, keepdims=True)


def tree_sum(terms):
    terms = list(terms)
    while len(terms) > 1:
        terms = [terms[k] + terms[k + 1] for k in range(0, len(terms), 2)]
    return terms[0]


def set_state(weight, total):
    lane = lax.broadcasted_iota(jnp.int32, (weight.shape[0], TAIL), 1)
    return jnp.where(lane == 0, weight, jnp.where(lane == 1, total, 0.0))


class Blocks:
    def __init__(self, order, slots, cols):
        self.order, self.slots, self.cols = order, slots, cols
        self.n = order[order.shape[0] - 1]

    def ready(self, spot):
        pass

    def run(self, body):
        def several(first, width):
            spots = [self.order[first + q] for q in range(width)]
            for spot in spots:
                self.ready(spot)
            for spot in spots:
                body(spot // self.cols, spot % self.cols, self.slots[spot])

        def four(u, carry):
            several(u * 4, 4)
            return carry

        lax.fori_loop(0, self.n // 4, four, 0)
        pl.when(self.n % 4 >= 2)(lambda: several(self.n // 4 * 4, 2))
        pl.when(self.n % 2 == 1)(lambda: several(self.n - 1, 1))

    def back(self, vector, acc):
        size_r, size_c = self.slots.shape[1:]
        acc[...] = jnp.zeros_like(acc)

        def body(i, j, block):
            rows = vector[:, pl.ds(pl.multiple_of(i * size_r, size_r), size_r)]
            acc[:, pl.ds(pl.multiple_of(j * size_c, size_c), size_c)] += jnp.dot(
                rows, block, preferred_element_type=f32
            )

        self.run(body)

    def forward(self, vector, acc):
        size_c, size_r = self.slots.shape[1:]
        acc[...] = jnp.zeros_like(acc)

        def body(i, j, block):
            cols = vector[:, pl.ds(pl.multiple_of(j * size_c, size_c), size_c)]
            acc[:, pl.ds(pl.multiple_of(i * size_r, size_r), size_r)] += jnp.dot(
                cols, block, preferred_element_type=f32
            )

        self.run(body)


class Incoming(Blocks):
    def __init__(self, tile_map, source, slots, sems, order, partner_flag=None):
        each, cols = tile_map.shape
        first_row = each if partner_flag else 0
        size_r, size_c = slots.shape[1:]
        n = jnp.int32(0)
        for i in range(each + first_row):
            for j in range(cols):
                spot = i * cols + j
                nonzero = tile_map[i, j] != 0 if i < each else partner_flag(spot - each * cols) != 0

                @pl.when(nonzero)
                def _():
                    order[n] = spot
                    if i >= first_row:
                        pltpu.make_async_copy(
                            source.at[pl.ds((i - first_row) * size_r, size_r), pl.ds(j * size_c, size_c)],
                            slots.at[spot],
                            sems.at[spot],
                        ).start()

                n = n + nonzero.astype(jnp.int32)
        order[order.shape[0] - 1] = n
        self.sems = sems
        super().__init__(order, slots, cols)
        self.n = n

    def ready(self, spot):
        pltpu.make_async_copy(self.slots.at[spot], self.slots.at[spot], self.sems.at[spot]).wait()


def first_kernel(tile_map, place, blocks, dual, cost, lower, upper, code, weights, *refs):
    mine, others, vectors = refs[0], refs[1 : 1 + BATCHES], refs[1 + BATCHES]
    states = refs[2 + BATCHES : 2 + 2 * BATCHES]
    slots, sems, order, vector, acc, start, sem = refs[2 + 2 * BATCHES :]
    fetch = pltpu.make_async_copy(dual, start, sem)
    fetch.start()
    incoming = Incoming(tile_map, blocks, slots, sems, order)
    width = mine.shape[0]
    size = width // BATCHES
    low_on = (code[...] == 1) | (code[...] == 3)
    high_on = (code[...] == 2) | (code[...] == 3)
    vectors[0:1] = cost[...]
    vectors[1:2] = jnp.where(low_on, lower[...], -jnp.inf)
    vectors[2:3] = jnp.where(high_on, upper[...], jnp.inf)
    here = pl.multiple_of(place[1] * width, width)
    column = jnp.broadcast_to(weights[:, pl.ds(here, width)], (TAIL, width)).T
    for b, state in enumerate(states):
        state[...] = column[b * size : (b + 1) * size]
    fetch.wait()
    vector[...] = start[...].T.astype(bf16)
    incoming.back(vector, acc)
    mine[...] = acc[pl.ds(here, width)]
    there = pl.multiple_of((1 - place[1]) * width, width)
    for b, other in enumerate(others):
        other[:size] = acc[pl.ds(there + b * size, size)]
    lane = lax.broadcasted_iota(jnp.int32, (8, vector.shape[1]), 1)
    flags = jnp.zeros(lane.shape, jnp.int32)
    for t in range(tile_map.shape[0] * tile_map.shape[1]):
        flags = jnp.where(lane == t, tile_map[t // tile_map.shape[1], t % tile_map.shape[1]], flags)
    others[0][size:, : lane.shape[1]] = flags.astype(f32)


def load_kernel(second, tile_map, source, *refs):
    slots, turned, order, sems = refs[-4:]
    partner_flag = None
    if second:
        partner_flag = lambda t: refs[0][refs[0].shape[0] - 8, t]
    incoming = Incoming(tile_map, source, slots, sems, order, partner_flag)
    first_row = tile_map.shape[0] if second else 0

    def one(q, carry):
        spot = order[q]

        @pl.when(spot >= first_row * incoming.cols)
        def _():
            incoming.ready(spot)
            turned[spot] = slots[spot].T

        return carry

    lax.fori_loop(0, incoming.n, one, 0)


def first_pack_kernel(batch, mine, other, after, msg):
    size = msg.shape[0]
    msg[...] = (mine[batch * size : (batch + 1) * size] + other[:size]).astype(bf16)


def back_kernel(grid_cols, order, place, own_half, got_half, slots, after, msg, *refs):
    vector, acc = refs[-2:]
    half = vector.shape[1] // 2
    side = place[0] % 2
    vector[:, pl.ds(pl.multiple_of(side * half, half), half)] = own_half[:, :half]
    vector[:, pl.ds(pl.multiple_of((1 - side) * half, half), half)] = got_half[:, :half]
    if len(refs) == 3:
        refs[0][...] = vector[:, half:]
    Blocks(order, slots, grid_cols).back(vector, acc)
    width = acc.shape[1]
    msg[:, :width] = acc[...].astype(bf16)
    tails = own_half[:, half:], got_half[:, half:]
    msg[:, width:] = split_sums(*[join_sum(tails[0], k) + join_sum(tails[1], k) for k in range(2)])


def forward_kernel(grid_cols, near, first, last, total_rows, total_cols, order, place, *refs):
    msgs = refs[:near]
    primal, vectors, state, turned, after_ref = refs[near : near + 5]
    primal_next, kept, sent, state_out, vector, acc = refs[near + 5 :]
    width = primal.shape[1]
    weight = state[:, 0:1]
    if not first:
        sum_y = tree_sum([join_sum(ref[:, width:]) for ref in msgs])
        move_y = jnp.sqrt(sum_y / total_rows + 1e-06)
        sum_x = join_sum(msgs[0][:, width:], 1)
        move_x = jnp.sqrt(sum_x / total_cols + 1e-06)
        weight = jnp.sqrt(weight * move_y / move_x)
    step = STEP_SCALE / weight
    image_t = tree_sum([ref[:, :width].astype(f32) for ref in msgs])
    before = primal[...]
    after = before - step * (vectors[0:1] - image_t)
    after = jnp.minimum(jnp.maximum(after, vectors[1:2]), vectors[2:3])
    primal_next[...] = after
    vector[...] = (2.0 * after - before).astype(bf16)
    sum_x = jnp.zeros_like(weight) if last else jnp.sum((after - before) ** 2, axis=1, keepdims=True)
    state_out[...] = set_state(weight, sum_x)
    Blocks(order, turned, grid_cols).forward(vector, acc)
    half = acc.shape[1] // 2
    side = place[0] % 2
    kept[...] = acc[:, pl.ds(pl.multiple_of(side * half, half), half)]
    sent[...] = acc[:, pl.ds(pl.multiple_of((1 - side) * half, half), half)].astype(bf16)


def pair_kernel(kept, state, got, after, msg):
    half = kept.shape[1]
    msg[:, :half] = (kept[...] + got[...].astype(f32)).astype(bf16)
    if msg.shape[1] > half:
        msg[:, half:] = split_sums(state[:, 1:2])


def cross_kernel(half, own, got, msg):
    msg[:, :half] = (own[:, :half].astype(f32) + got[:, :half].astype(f32)).astype(bf16)
    if msg.shape[1] > half:
        msg[:, half:] = split_sums(join_sum(own[:, half:]) + join_sum(got[:, half:]))


def dual_kernel(last, own, got, state, dual, right, floor, before_ref, after_ref, dual_next, msg):
    half = dual.shape[1]
    image = own[:, :half].astype(f32) + got[:, :half].astype(f32)
    before = dual[...]
    after = before + STEP_SCALE * state[:, 0:1] * (right[...] - image)
    after = jnp.maximum(after, floor[0:1])
    if last:
        rounded = before_ref[:, :half].astype(f32)
        step = (after - rounded).astype(bf16)
        msg[...] = step
        dual_next[...] = rounded + step.astype(f32)
    else:
        dual_next[...] = after
        msg[:, :half] = after.astype(bf16)
        sum_y = jnp.sum((after - before) ** 2, axis=1, keepdims=True)
        msg[:, half:] = split_sums(sum_y, join_sum(own[:, half:]) + join_sum(got[:, half:]))


def turn_kernel(place, value, after, *refs):
    outs, (held, sem) = refs[:BATCHES], refs[BATCHES:]
    size = outs[0].shape[0]
    width = size * BATCHES
    fetch = pltpu.make_async_copy(value.at[:, pl.ds(pl.multiple_of(place[1] * width, width), width)], held, sem)
    fetch.start()
    fetch.wait()
    turned = held[...].T
    for b, out in enumerate(outs):
        out[...] = turned[b * size : (b + 1) * size]


def rows_kernel(place, dual, right, kind, got_dual, got_right, got_kind, after, floor, *refs):
    outs, (held, sems) = refs[: 2 * BATCHES], refs[2 * BATCHES :]
    size = outs[0].shape[0]
    width = size * BATCHES
    rows = dual.shape[0]
    here = pl.ds(pl.multiple_of(place[1] * width, width), width)

    def put(dual, right, kind):
        copies = [
            pltpu.make_async_copy(dual.at[:, here], held.at[pl.ds(0, rows)], sems.at[0]),
            pltpu.make_async_copy(right.at[:, here], held.at[pl.ds(rows, rows)], sems.at[1]),
        ]
        for copy in copies:
            copy.start()
        floor[...] = jnp.where(kind[...] == 1, 0.0, -jnp.inf)
        for k, copy in enumerate(copies):
            copy.wait()
            turned = held[k * rows : (k + 1) * rows].T
            for b in range(BATCHES):
                outs[k * BATCHES + b][...] = turned[b * size : (b + 1) * size]

    pl.when(place[0] % 2 == 0)(lambda: put(dual, right, kind))
    pl.when(place[0] % 2 == 1)(lambda: put(got_dual, got_right, got_kind))


def put_half(out, core, parts):
    width = out.shape[1] // 2
    out[:, pl.ds(pl.multiple_of(core * width, width), width)] = jnp.concatenate([r[...] for r in parts], axis=0).T


def primal_out_kernel(place, *refs):
    mine, theirs, (out, token) = refs[:BATCHES], refs[BATCHES : 2 * BATCHES], refs[-2:]
    token[...] = jnp.zeros_like(token)
    put_half(out, place[1], mine)
    put_half(out, 1 - place[1], theirs)


def dual_out_kernel(place, own, got_step, partner_step, got_before, partner_before, after, *refs):
    out = refs[-1]

    def put(mine, theirs):
        rows = jnp.concatenate([mine(), theirs()], axis=0).T
        if len(refs) == 1:
            out[...] = rows
            return
        before = refs[0][...]
        width = before.shape[1]
        low = lax.broadcasted_iota(jnp.int32, before.shape, 1) < width // 2
        out[:, pl.ds(pl.multiple_of(place[1] * width, width), width)] = jnp.where(
            low, before, pltpu.roll(rows, width // 2, 1)
        )
        out[:, pl.ds(pl.multiple_of((1 - place[1]) * width, width), width)] = jnp.where(
            low, pltpu.roll(before, width // 2, 1), rows
        )

    def moved(before, step):
        return before[:, : step.shape[1]].astype(f32) + step[...].astype(f32)

    even = (lambda: own[...]), (lambda: moved(partner_before, got_step))
    odd = (lambda: moved(got_before, got_step)), (lambda: moved(partner_before, partner_step))
    pl.when(place[0] % 2 == 0)(lambda: put(*even))
    pl.when(place[0] % 2 == 1)(lambda: put(*odd))


def call(kernel, out_shape, in_specs, scratch=(), flops=0, name=None, vmem=6, out_specs=None):
    return pl.pallas_call(
        kernel,
        out_shape=out_shape,
        in_specs=in_specs,
        out_specs=out_specs or jax.tree.map(lambda _: VMEM, out_shape),
        scratch_shapes=list(scratch),
        compiler_params=pltpu.CompilerParams(vmem_limit_bytes=vmem << 20),
        cost_estimate=pl.CostEstimate(flops=flops, bytes_accessed=0, transcendentals=0),
        name=name,
    )


def shape(rows, cols, kind=f32):
    return jax.ShapeDtypeStruct((rows, cols), kind)


def local(
    blocks,
    tile_map,
    lower_bound,
    upper_bound,
    bound_code,
    row_kind,
    cost_vector,
    right_side,
    primal_start,
    dual_start,
    primal_weight,
):
    rows, cols = blocks.shape
    size_r = rows // tile_map.shape[0]
    size_c = cols // tile_map.shape[1]
    profiles = dual_start.shape[1]
    width = profiles // 2
    size = width // BATCHES
    count = lax.axis_size("col")
    near = lax.axis_size("row") // 2
    total_rows = rows * near * 2
    total_cols = cols * count
    z = lax.axis_index("col")
    core = lax.axis_index("row") % 2
    place = jnp.stack([z, core]).astype(jnp.int32)

    def to_core(value):
        return lax.ppermute(value, "row", [(i, i ^ 1) for i in range(2 * near)])

    def to_x(value, k):
        return lax.ppermute(value, "row", [(i, i ^ (2 * k)) for i in range(2 * near)])

    def to_z(value, k):
        return lax.ppermute(value, "col", [(i, i ^ k) for i in range(count)])

    to_holder = [
        (r * count + c, (r ^ (c % 2)) * count + (c ^ 1)) for r in range(2 * near) for c in range(count)
    ]

    n_own = tile_map.size
    n_chip = 2 * n_own
    grid_cols = tile_map.shape[1]

    blocks, tile_map, primal_start, dual_start, right_side = (
        pltpu.with_memory_space_constraint(value, pltpu.HBM)
        for value in (blocks, tile_map, primal_start, dual_start, right_side)
    )
    vectors = [
        pltpu.with_memory_space_constraint(value[None, :], pltpu.HBM)
        for value in (cost_vector, lower_bound, upper_bound, bound_code, primal_weight)
    ]
    partner = to_core(blocks)
    mine, *rest = call(
        first_kernel,
        (shape(width, cols),)
        + (shape(size + 8, cols),)
        + (shape(size, cols),) * (BATCHES - 1)
        + (shape(8, cols),)
        + (shape(size, TAIL),) * BATCHES,
        [SMEM, SMEM, HBM, HBM] + [VMEM] * 5,
        [
            pltpu.VMEM((n_own, size_r, size_c), bf16),
            pltpu.SemaphoreType.DMA((n_own,)),
            pltpu.SMEM((n_own + 1,), jnp.int32),
            pltpu.VMEM((profiles, rows), bf16),
            pltpu.VMEM((profiles, cols), f32),
            pltpu.VMEM((rows, profiles), f32),
            pltpu.SemaphoreType.DMA,
        ],
        name="first_product",
        vmem=20,
    )(
        tile_map,
        place,
        blocks,
        dual_start,
        *vectors,
    )
    others = [to_core(other) for other in rest[:BATCHES]]
    vectors, state = rest[BATCHES], list(rest[BATCHES + 1 :])
    sides = dual_start, right_side, row_kind[None, :]
    sides += tuple(to_core(value) for value in sides)

    def half_msg(tail):
        return shape(size, rows + (TAIL if tail else 0), bf16)

    def back(b, iteration, after):
        if iteration == 0:
            messages[b] = call(
                functools.partial(first_pack_kernel, b),
                shape(size, cols, bf16),
                [VMEM] * 2 + [ANY],
                flops=STAGE_FLOPS,
                name="first_pack",
            )(mine, others[b], after)
        else:
            last = iteration + 1 == ITERS
            outs = call(
                functools.partial(back_kernel, grid_cols),
                (shape(size, cols + TAIL, bf16),) + (half_msg(False),) * last,
                [SMEM, SMEM, VMEM, VMEM, VMEM, ANY],
                [pltpu.VMEM((size, 2 * rows), bf16), pltpu.VMEM((size, cols), f32)],
                flops=STAGE_FLOPS,
                name="back_product",
            )(order, place, *halves[b], slots, after)
            messages[b] = outs[0]
            if last:
                partner_before[b] = to_core(outs[1])
        return messages[b]

    def forward(b, iteration, after):
        first, last = iteration == 0, iteration + 1 == ITERS
        msgs = [messages[b]] + [to_x(messages[b], k) for k in range(1, near)]
        outs = call(
            functools.partial(forward_kernel, grid_cols, near, first, last, total_rows, total_cols),
            (shape(size, cols), shape(size, rows), half_msg(False), shape(size, TAIL)),
            [SMEM, SMEM] + [VMEM] * (near + 4) + [ANY],
            [pltpu.VMEM((size, cols), bf16), pltpu.VMEM((size, 2 * rows), f32)],
            flops=STAGE_FLOPS,
            name="forward_product",
        )(order, place, *msgs, primal[b], vectors, state[b], turned, after)
        primal[b], kept[b], sent[b], state[b] = outs
        return state[b]

    def pair(b, iteration, after):
        out = half_msg(iteration + 1 < ITERS)
        crossing[b] = call(pair_kernel, out, [VMEM] * 3 + [ANY], flops=STAGE_FLOPS, name="pair_sum")(
            kept[b], state[b], to_z(sent[b], 1), after
        )
        mask = 2
        while mask * 2 < count:
            crossing[b] = call(functools.partial(cross_kernel, rows), out, [VMEM] * 2, name="cross_sum")(
                crossing[b], to_z(crossing[b], mask)
            )
            mask *= 2
        return crossing[b]

    def update(b, iteration, after):
        last = iteration + 1 == ITERS
        got = to_z(crossing[b], count // 2)
        dual[b], msg = call(
            functools.partial(dual_kernel, last),
            (shape(size, rows), half_msg(not last)),
            [VMEM] * 6 + [VMEM if last else ANY, ANY],
            flops=STAGE_FLOPS,
            name="dual_update",
        )(crossing[b], got, state[b], dual[b], right[b], floor, halves[b][0] if last else after, after)
        if last:
            steps[b] = lax.ppermute(msg, ("row", "col"), to_holder), to_core(msg)
        else:
            halves[b] = msg, to_z(msg, 1)
        return msg

    plan = []
    for b in range(BATCHES):
        at = b * LAG
        for iteration in range(ITERS):
            for stage in (back, forward, pair, update):
                plan.append((at, b, iteration, stage))
                at += 1
    plan.sort(key=lambda entry: entry[:3])

    messages, halves, kept, sent, crossing, steps, partner_before = ([None] * BATCHES for _ in range(7))
    loaded = (
        pltpu.VMEM((n_chip, size_r, size_c), bf16),
        pltpu.VMEM((n_chip, size_c, size_r), bf16),
        jax.ShapeDtypeStruct((n_chip + 1,), jnp.int32),
    )

    def load(second, source, operands, in_specs, aliases):
        return pl.pallas_call(
            functools.partial(load_kernel, second),
            out_shape=loaded,
            in_specs=[SMEM, HBM] + in_specs,
            out_specs=(VMEM, VMEM, SMEM),
            scratch_shapes=[pltpu.SemaphoreType.DMA((n_chip,))],
            input_output_aliases=aliases,
            compiler_params=pltpu.CompilerParams(vmem_limit_bytes=4 << 20),
            cost_estimate=pl.CostEstimate(flops=0, bytes_accessed=0, transcendentals=0),
            name="load_blocks",
        )(tile_map, source, *operands)

    plan = [(b, iteration, stage) for _, b, iteration, stage in plan]
    primal = list(
        call(
            turn_kernel,
            (shape(size, cols),) * BATCHES,
            [SMEM, HBM, ANY],
            [pltpu.VMEM((cols, width), f32), pltpu.SemaphoreType.DMA],
            name="turn_primal",
        )(place, primal_start, state[0])
    )
    token = primal[0]
    for b, iteration, stage in plan:
        token = stage(b, iteration, token)
        if (b, iteration, stage) == (0, 0, back):
            slots, turned, order = load(False, blocks, (token,), [ANY], {})
            slots, turned, order = load(
                True, partner, (others[0], slots, turned), [VMEM, ANY, ANY], {3: 0, 4: 1}
            )
        if (b, iteration, stage) == (0, 0, forward):
            floor, *held = call(
                rows_kernel,
                (shape(1, rows),) + (shape(size, rows),) * (2 * BATCHES),
                [SMEM] + [HBM, HBM, VMEM] * 2 + [ANY],
                [pltpu.VMEM((2 * rows, width), f32), pltpu.SemaphoreType.DMA((2,))],
                name="turn_rows",
            )(place, *sides, token)
            dual, right = held[:BATCHES], held[BATCHES:]
        if (b, iteration, stage) == (BATCHES - 1, ITERS - 1, pair):
            primal_final, token = call(
                primal_out_kernel,
                (pltpu.HBM((cols, profiles), f32), shape(8, TAIL)),
                [SMEM] + [VMEM] * (2 * BATCHES) + [ANY],
                name="primal_out",
            )(place, *primal, *[to_core(p) for p in primal], token)

    def dual_out(b, out_shape, flops, name, *others):
        return call(
            dual_out_kernel, out_shape, [SMEM] + [VMEM] * 5 + [ANY] + [VMEM] * len(others), flops=flops, name=name
        )(place, dual[b], *steps[b], halves[b][1], partner_before[b], token, *others)

    first_rows = dual_out(0, shape(rows, 2 * size), STAGE_FLOPS, "dual_part")
    dual_final = dual_out(1, shape(rows, profiles), 0, "dual_out", first_rows)
    return primal_final, dual_final


def solution(mesh):
    return jax.shard_map(
        local,
        mesh=mesh,
        in_specs=(
            P("row", "col"),
            P("row", "col"),
            P("col"),
            P("col"),
            P("col"),
            P("row"),
            P("col"),
            P("row", "groups"),
            P("col", "groups"),
            P("row", "groups"),
            P("groups"),
        ),
        out_specs=(P("col", "groups"), P("row", "groups")),
        check_vma=False,
    )
```

```python
import functools

import jax
import jax.numpy as jnp
from jax import lax
from jax.experimental import pallas as pl
from jax.experimental.pallas import tpu as pltpu
from jax.sharding import PartitionSpec as P

ITERS = 3
STEP_SCALE = 0.5
BATCHES = 2
LAG = 1
STAGE_FLOPS = 4 * 10**9
TAIL = 128

bf16 = jnp.bfloat16
f32 = jnp.float32

SMEM = pl.BlockSpec(memory_space=pltpu.SMEM)
VMEM = pl.BlockSpec(memory_space=pltpu.VMEM)
ANY = pl.BlockSpec(memory_space=pl.ANY)
HBM = pl.BlockSpec(memory_space=pltpu.HBM)


def split_sums(*totals):
    lane = lax.broadcasted_iota(jnp.int32, (totals[0].shape[0], TAIL), 1)
    block = jnp.zeros(lane.shape, f32)
    for k, rest in enumerate(totals):
        for part in range(3):
            rounded = rest.astype(bf16).astype(f32)
            block = jnp.where(lane == 3 * k + part, rounded, block)
            rest = rest - rounded
    return block.astype(bf16)


def join_sum(block, k=0):
    lane = lax.broadcasted_iota(jnp.int32, block.shape, 1)
    mine = (lane >= 3 * k) & (lane < 3 * k + 3)
    return jnp.sum(jnp.where(mine, block.astype(f32), 0.0), axis=1, keepdims=True)


def tree_sum(terms):
    terms = list(terms)
    while len(terms) > 1:
        terms = [terms[k] + terms[k + 1] for k in range(0, len(terms), 2)]
    return terms[0]


def set_state(weight, total):
    lane = lax.broadcasted_iota(jnp.int32, (weight.shape[0], TAIL), 1)
    return jnp.where(lane == 0, weight, jnp.where(lane == 1, total, 0.0))


class Blocks:
    def __init__(self, order, slots, cols):
        self.order, self.slots, self.cols = order, slots, cols
        self.n = order[order.shape[0] - 1]

    def ready(self, spot):
        pass

    def run(self, body):
        def several(first, width):
            spots = [self.order[first + q] for q in range(width)]
            for spot in spots:
                self.ready(spot)
            for spot in spots:
                body(spot // self.cols, spot % self.cols, self.slots[spot])

        def four(u, carry):
            several(u * 4, 4)
            return carry

        lax.fori_loop(0, self.n // 4, four, 0)
        pl.when(self.n % 4 >= 2)(lambda: several(self.n // 4 * 4, 2))
        pl.when(self.n % 2 == 1)(lambda: several(self.n - 1, 1))

    def back(self, vector, acc):
        size_r, size_c = self.slots.shape[1:]
        acc[...] = jnp.zeros_like(acc)

        def body(i, j, block):
            rows = vector[:, pl.ds(pl.multiple_of(i * size_r, size_r), size_r)]
            acc[:, pl.ds(pl.multiple_of(j * size_c, size_c), size_c)] += jnp.dot(
                rows, block, preferred_element_type=f32
            )

        self.run(body)

    def forward(self, vector, acc):
        size_c, size_r = self.slots.shape[1:]
        acc[...] = jnp.zeros_like(acc)

        def body(i, j, block):
            cols = vector[:, pl.ds(pl.multiple_of(j * size_c, size_c), size_c)]
            acc[:, pl.ds(pl.multiple_of(i * size_r, size_r), size_r)] += jnp.dot(
                cols, block, preferred_element_type=f32
            )

        self.run(body)


class Incoming(Blocks):
    def __init__(self, tile_map, source, slots, sems, order, partner_flag=None):
        each, cols = tile_map.shape
        first_row = each if partner_flag else 0
        size_r, size_c = slots.shape[1:]
        n = jnp.int32(0)
        for i in range(each + first_row):
            for j in range(cols):
                spot = i * cols + j
                nonzero = tile_map[i, j] != 0 if i < each else partner_flag(spot - each * cols) != 0

                @pl.when(nonzero)
                def _():
                    order[n] = spot
                    if i >= first_row:
                        pltpu.make_async_copy(
                            source.at[pl.ds((i - first_row) * size_r, size_r), pl.ds(j * size_c, size_c)],
                            slots.at[spot],
                            sems.at[spot],
                        ).start()

                n = n + nonzero.astype(jnp.int32)
        order[order.shape[0] - 1] = n
        self.sems = sems
        super().__init__(order, slots, cols)
        self.n = n

    def ready(self, spot):
        pltpu.make_async_copy(self.slots.at[spot], self.slots.at[spot], self.sems.at[spot]).wait()


def first_kernel(tile_map, place, blocks, dual, cost, lower, upper, code, weights, kind, *refs):
    mine, others, vectors = refs[0], refs[1 : 1 + BATCHES], refs[1 + BATCHES]
    states = refs[2 + BATCHES : 2 + 2 * BATCHES]
    slots, sems, order, vector, acc, start, sem = refs[2 + 2 * BATCHES :]
    fetch = pltpu.make_async_copy(dual, start, sem)
    fetch.start()
    incoming = Incoming(tile_map, blocks, slots, sems, order)
    width = mine.shape[0]
    size = width // BATCHES
    low_on = (code[...] == 1) | (code[...] == 3)
    high_on = (code[...] == 2) | (code[...] == 3)
    vectors[0:1] = cost[...]
    vectors[1:2] = jnp.where(low_on, lower[...], -jnp.inf)
    vectors[2:3] = jnp.where(high_on, upper[...], jnp.inf)
    here = pl.multiple_of(place[1] * width, width)
    column = jnp.broadcast_to(weights[:, pl.ds(here, width)], (TAIL, width)).T
    for b, state in enumerate(states):
        state[...] = column[b * size : (b + 1) * size]
    fetch.wait()
    vector[...] = start[...].T.astype(bf16)
    incoming.back(vector, acc)
    mine[...] = acc[pl.ds(here, width)]
    there = pl.multiple_of((1 - place[1]) * width, width)
    for b, other in enumerate(others):
        other[:size] = acc[pl.ds(there + b * size, size)]
    lane = lax.broadcasted_iota(jnp.int32, (8, vector.shape[1]), 1)
    flags = jnp.zeros(lane.shape, jnp.int32)
    for t in range(tile_map.shape[0] * tile_map.shape[1]):
        flags = jnp.where(lane == t, tile_map[t // tile_map.shape[1], t % tile_map.shape[1]], flags)
    flags = jnp.where(lax.broadcasted_iota(jnp.int32, lane.shape, 0) == 1, kind[...], flags)
    others[0][size:, : lane.shape[1]] = flags.astype(f32)


def load_kernel(second, tile_map, source, *refs):
    slots, turned, order, sems = refs[-4:]
    partner_flag = None
    if second:
        partner_flag = lambda t: refs[0][refs[0].shape[0] - 8, t]
    incoming = Incoming(tile_map, source, slots, sems, order, partner_flag)
    first_row = tile_map.shape[0] if second else 0

    def one(q, carry):
        spot = order[q]

        @pl.when(spot >= first_row * incoming.cols)
        def _():
            incoming.ready(spot)
            turned[spot] = slots[spot].T

        return carry

    lax.fori_loop(0, incoming.n, one, 0)


def first_pack_kernel(batch, mine, other, after, msg):
    size = msg.shape[0]
    msg[...] = (mine[batch * size : (batch + 1) * size] + other[:size]).astype(bf16)


def back_kernel(grid_cols, order, place, own_half, got_half, slots, after, msg, *refs):
    vector, acc = refs[-2:]
    half = vector.shape[1] // 2
    side = place[0] % 2
    vector[:, pl.ds(pl.multiple_of(side * half, half), half)] = own_half[:, :half]
    vector[:, pl.ds(pl.multiple_of((1 - side) * half, half), half)] = got_half[:, :half]
    if len(refs) == 3:
        refs[0][...] = vector[:, half:]
    Blocks(order, slots, grid_cols).back(vector, acc)
    width = acc.shape[1]
    msg[:, :width] = acc[...].astype(bf16)
    tails = own_half[:, half:], got_half[:, half:]
    msg[:, width:] = split_sums(*[join_sum(tails[0], k) + join_sum(tails[1], k) for k in range(2)])


def forward_kernel(grid_cols, near, first, last, total_rows, total_cols, order, place, *refs):
    msgs = refs[:near]
    primal, vectors, state, turned, after_ref = refs[near : near + 5]
    primal_next, kept, sent, state_out, vector, acc = refs[near + 5 :]
    width = primal.shape[1]
    weight = state[:, 0:1]
    if not first:
        sum_y = tree_sum([join_sum(ref[:, width:]) for ref in msgs])
        move_y = jnp.sqrt(sum_y / total_rows + 1e-06)
        sum_x = join_sum(msgs[0][:, width:], 1)
        move_x = jnp.sqrt(sum_x / total_cols + 1e-06)
        weight = jnp.sqrt(weight * move_y / move_x)
    step = STEP_SCALE / weight
    image_t = tree_sum([ref[:, :width].astype(f32) for ref in msgs])
    before = primal[...]
    after = before - step * (vectors[0:1] - image_t)
    after = jnp.minimum(jnp.maximum(after, vectors[1:2]), vectors[2:3])
    primal_next[...] = after
    vector[...] = (2.0 * after - before).astype(bf16)
    sum_x = jnp.zeros_like(weight) if last else jnp.sum((after - before) ** 2, axis=1, keepdims=True)
    state_out[...] = set_state(weight, sum_x)
    Blocks(order, turned, grid_cols).forward(vector, acc)
    half = acc.shape[1] // 2
    side = place[0] % 2
    kept[...] = acc[:, pl.ds(pl.multiple_of(side * half, half), half)]
    sent[...] = acc[:, pl.ds(pl.multiple_of((1 - side) * half, half), half)].astype(bf16)


def pair_kernel(kept, state, got, after, msg):
    half = kept.shape[1]
    msg[:, :half] = (kept[...] + got[...].astype(f32)).astype(bf16)
    if msg.shape[1] > half:
        msg[:, half:] = split_sums(state[:, 1:2])


def cross_kernel(half, own, got, msg):
    msg[:, :half] = (own[:, :half].astype(f32) + got[:, :half].astype(f32)).astype(bf16)
    if msg.shape[1] > half:
        msg[:, half:] = split_sums(join_sum(own[:, half:]) + join_sum(got[:, half:]))


def dual_kernel(last, own, got, state, dual, right, floor, before_ref, after_ref, dual_next, msg):
    half = dual.shape[1]
    image = own[:, :half].astype(f32) + got[:, :half].astype(f32)
    before = dual[...]
    after = before + STEP_SCALE * state[:, 0:1] * (right[...] - image)
    after = jnp.maximum(after, floor[0:1])
    if last:
        rounded = before_ref[:, :half].astype(f32)
        step = (after - rounded).astype(bf16)
        msg[...] = step
        dual_next[...] = rounded + step.astype(f32)
    else:
        dual_next[...] = after
        msg[:, :half] = after.astype(bf16)
        sum_y = jnp.sum((after - before) ** 2, axis=1, keepdims=True)
        msg[:, half:] = split_sums(sum_y, join_sum(own[:, half:]) + join_sum(got[:, half:]))


def turn_kernel(place, value, after, *refs):
    outs, (held, sem) = refs[:BATCHES], refs[BATCHES:]
    size = outs[0].shape[0]
    width = size * BATCHES
    fetch = pltpu.make_async_copy(value.at[:, pl.ds(pl.multiple_of(place[1] * width, width), width)], held, sem)
    fetch.start()
    fetch.wait()
    turned = held[...].T
    for b, out in enumerate(outs):
        out[...] = turned[b * size : (b + 1) * size]


def rows_kernel(place, dual, right, got_dual, got_right, kind, other, after, floor, *refs):
    outs, (held, sems) = refs[: 2 * BATCHES], refs[2 * BATCHES :]
    size = outs[0].shape[0]
    width = size * BATCHES
    rows = dual.shape[0]
    here = pl.ds(pl.multiple_of(place[1] * width, width), width)

    def put(dual, right, one_sided):
        copies = [
            pltpu.make_async_copy(dual.at[:, here], held.at[pl.ds(0, rows)], sems.at[0]),
            pltpu.make_async_copy(right.at[:, here], held.at[pl.ds(rows, rows)], sems.at[1]),
        ]
        for copy in copies:
            copy.start()
        floor[...] = jnp.where(one_sided, 0.0, -jnp.inf)
        for k, copy in enumerate(copies):
            copy.wait()
            turned = held[k * rows : (k + 1) * rows].T
            for b in range(BATCHES):
                outs[k * BATCHES + b][...] = turned[b * size : (b + 1) * size]

    pl.when(place[0] % 2 == 0)(lambda: put(dual, right, kind[...] == 1))
    pl.when(place[0] % 2 == 1)(lambda: put(got_dual, got_right, other[size + 1 : size + 2, :rows] == 1.0))


def put_half(out, core, parts):
    width = out.shape[1] // 2
    out[:, pl.ds(pl.multiple_of(core * width, width), width)] = jnp.concatenate([r[...] for r in parts], axis=0).T


def primal_out_kernel(place, *refs):
    mine, theirs, (out, token) = refs[:BATCHES], refs[BATCHES : 2 * BATCHES], refs[-2:]
    token[...] = jnp.zeros_like(token)
    put_half(out, place[1], mine)
    put_half(out, 1 - place[1], theirs)


def last_rows(place, own, got_step, partner_step, got_before, partner_before):
    rows = own.shape[1]
    even = place[0] % 2 == 0
    step = got_step[...].astype(f32)
    mine = jnp.where(even, own[...], got_before[:, :rows].astype(f32) + step)
    return mine, partner_before[...].astype(f32) + jnp.where(even, step, partner_step[...].astype(f32))


def dual_part_kernel(place, *refs):
    refs[-1][...] = jnp.concatenate(last_rows(place, *refs[:5]), axis=0).T


def dual_out_kernel(place, *refs):
    part, out, block, sems = refs[-4:]
    both = jnp.concatenate(last_rows(place, *refs[:5]), axis=0)
    rows, width = part.shape
    chunk = rows // sems.shape[0]
    low = lax.broadcasted_iota(jnp.int32, (chunk, width), 1) < width // 2
    copies = []
    for k in range(sems.shape[0]):
        here = pl.ds(k * chunk, chunk)
        before = part[here]
        turned = both[:, k * chunk : (k + 1) * chunk].T
        block[here, pl.ds(pl.multiple_of(place[1] * width, width), width)] = jnp.where(
            low, before, pltpu.roll(turned, width // 2, 1)
        )
        block[here, pl.ds(pl.multiple_of((1 - place[1]) * width, width), width)] = jnp.where(
            low, pltpu.roll(before, width // 2, 1), turned
        )
        copies.append(pltpu.make_async_copy(block.at[here], out.at[here], sems.at[k]))
        copies[-1].start()
    for copy in copies:
        copy.wait()


def call(kernel, out_shape, in_specs, scratch=(), flops=0, name=None, vmem=6, out_specs=None):
    return pl.pallas_call(
        kernel,
        out_shape=out_shape,
        in_specs=in_specs,
        out_specs=out_specs or jax.tree.map(lambda _: VMEM, out_shape),
        scratch_shapes=list(scratch),
        compiler_params=pltpu.CompilerParams(vmem_limit_bytes=vmem << 20),
        cost_estimate=pl.CostEstimate(flops=flops, bytes_accessed=0, transcendentals=0),
        name=name,
    )


def shape(rows, cols, kind=f32):
    return jax.ShapeDtypeStruct((rows, cols), kind)


def local(
    blocks,
    tile_map,
    lower_bound,
    upper_bound,
    bound_code,
    row_kind,
    cost_vector,
    right_side,
    primal_start,
    dual_start,
    primal_weight,
):
    rows, cols = blocks.shape
    size_r = rows // tile_map.shape[0]
    size_c = cols // tile_map.shape[1]
    profiles = dual_start.shape[1]
    width = profiles // 2
    size = width // BATCHES
    count = lax.axis_size("col")
    near = lax.axis_size("row") // 2
    total_rows = rows * near * 2
    total_cols = cols * count
    z = lax.axis_index("col")
    core = lax.axis_index("row") % 2
    place = jnp.stack([z, core]).astype(jnp.int32)

    def to_core(value):
        return lax.ppermute(value, "row", [(i, i ^ 1) for i in range(2 * near)])

    def to_x(value, k):
        return lax.ppermute(value, "row", [(i, i ^ (2 * k)) for i in range(2 * near)])

    def to_z(value, k):
        return lax.ppermute(value, "col", [(i, i ^ k) for i in range(count)])

    to_holder = [
        (r * count + c, (r ^ (c % 2)) * count + (c ^ 1)) for r in range(2 * near) for c in range(count)
    ]

    n_own = tile_map.size
    n_chip = 2 * n_own
    grid_cols = tile_map.shape[1]

    blocks, tile_map, primal_start, dual_start, right_side = (
        pltpu.with_memory_space_constraint(value, pltpu.HBM)
        for value in (blocks, tile_map, primal_start, dual_start, right_side)
    )
    vectors_in = [
        pltpu.with_memory_space_constraint(value[None, :], pltpu.HBM)
        for value in (cost_vector, lower_bound, upper_bound, bound_code, primal_weight, row_kind)
    ]
    partner = to_core(blocks)
    mine, *rest = call(
        first_kernel,
        (shape(width, cols),)
        + (shape(size + 8, cols),)
        + (shape(size, cols),) * (BATCHES - 1)
        + (shape(8, cols),)
        + (shape(size, TAIL),) * BATCHES,
        [SMEM, SMEM, HBM, HBM] + [VMEM] * 6,
        [
            pltpu.VMEM((n_own, size_r, size_c), bf16),
            pltpu.SemaphoreType.DMA((n_own,)),
            pltpu.SMEM((n_own + 1,), jnp.int32),
            pltpu.VMEM((profiles, rows), bf16),
            pltpu.VMEM((profiles, cols), f32),
            pltpu.VMEM((rows, profiles), f32),
            pltpu.SemaphoreType.DMA,
        ],
        name="first_product",
        vmem=20,
    )(
        tile_map,
        place,
        blocks,
        dual_start,
        *vectors_in,
    )
    others = [to_core(other) for other in rest[:BATCHES]]
    vectors, state = rest[BATCHES], list(rest[BATCHES + 1 :])
    sides = dual_start, right_side, to_core(dual_start), to_core(right_side)

    def half_msg(tail):
        return shape(size, rows + (TAIL if tail else 0), bf16)

    def back(b, iteration, after):
        if iteration == 0:
            messages[b] = call(
                functools.partial(first_pack_kernel, b),
                shape(size, cols, bf16),
                [VMEM] * 2 + [ANY],
                flops=STAGE_FLOPS,
                name="first_pack",
            )(mine, others[b], after)
        else:
            last = iteration + 1 == ITERS
            outs = call(
                functools.partial(back_kernel, grid_cols),
                (shape(size, cols + TAIL, bf16),) + (half_msg(False),) * last,
                [SMEM, SMEM, VMEM, VMEM, VMEM, ANY],
                [pltpu.VMEM((size, 2 * rows), bf16), pltpu.VMEM((size, cols), f32)],
                flops=STAGE_FLOPS,
                name="back_product",
            )(order, place, *halves[b], slots, after)
            messages[b] = outs[0]
            if last:
                partner_before[b] = to_core(outs[1])
        return messages[b]

    def forward(b, iteration, after):
        first, last = iteration == 0, iteration + 1 == ITERS
        msgs = [messages[b]] + [to_x(messages[b], k) for k in range(1, near)]
        outs = call(
            functools.partial(forward_kernel, grid_cols, near, first, last, total_rows, total_cols),
            (shape(size, cols), shape(size, rows), half_msg(False), shape(size, TAIL)),
            [SMEM, SMEM] + [VMEM] * (near + 4) + [ANY],
            [pltpu.VMEM((size, cols), bf16), pltpu.VMEM((size, 2 * rows), f32)],
            flops=STAGE_FLOPS,
            name="forward_product",
        )(order, place, *msgs, primal[b], vectors, state[b], turned, after)
        primal[b], kept[b], sent[b], state[b] = outs
        return state[b]

    def pair(b, iteration, after):
        out = half_msg(iteration + 1 < ITERS)
        crossing[b] = call(pair_kernel, out, [VMEM] * 3 + [ANY], flops=STAGE_FLOPS, name="pair_sum")(
            kept[b], state[b], to_z(sent[b], 1), after
        )
        mask = 2
        while mask * 2 < count:
            crossing[b] = call(functools.partial(cross_kernel, rows), out, [VMEM] * 2, name="cross_sum")(
                crossing[b], to_z(crossing[b], mask)
            )
            mask *= 2
        return crossing[b]

    def update(b, iteration, after):
        last = iteration + 1 == ITERS
        got = to_z(crossing[b], count // 2)
        dual[b], msg = call(
            functools.partial(dual_kernel, last),
            (shape(size, rows), half_msg(not last)),
            [VMEM] * 6 + [VMEM if last else ANY, ANY],
            flops=STAGE_FLOPS,
            name="dual_update",
        )(crossing[b], got, state[b], dual[b], right[b], floor, halves[b][0] if last else after, after)
        if last:
            steps[b] = lax.ppermute(msg, ("row", "col"), to_holder), to_core(msg)
        else:
            halves[b] = msg, to_z(msg, 1)
        return msg

    plan = []
    for b in range(BATCHES):
        at = b * LAG
        for iteration in range(ITERS):
            for stage in (back, forward, pair, update):
                plan.append((at, b, iteration, stage))
                at += 1
    plan.sort(key=lambda entry: entry[:3])

    messages, halves, kept, sent, crossing, steps, partner_before = ([None] * BATCHES for _ in range(7))
    loaded = (
        pltpu.VMEM((n_chip, size_r, size_c), bf16),
        pltpu.VMEM((n_chip, size_c, size_r), bf16),
        jax.ShapeDtypeStruct((n_chip + 1,), jnp.int32),
    )

    def load(second, source, operands, in_specs, aliases):
        return pl.pallas_call(
            functools.partial(load_kernel, second),
            out_shape=loaded,
            in_specs=[SMEM, HBM] + in_specs,
            out_specs=(VMEM, VMEM, SMEM),
            scratch_shapes=[pltpu.SemaphoreType.DMA((n_chip,))],
            input_output_aliases=aliases,
            compiler_params=pltpu.CompilerParams(vmem_limit_bytes=4 << 20),
            cost_estimate=pl.CostEstimate(flops=0, bytes_accessed=0, transcendentals=0),
            name="load_blocks",
        )(tile_map, source, *operands)

    plan = [(b, iteration, stage) for _, b, iteration, stage in plan]
    primal = list(
        call(
            turn_kernel,
            (shape(size, cols),) * BATCHES,
            [SMEM, HBM, ANY],
            [pltpu.VMEM((cols, width), f32), pltpu.SemaphoreType.DMA],
            name="turn_primal",
        )(place, primal_start, state[0])
    )
    token = primal[0]
    for b, iteration, stage in plan:
        token = stage(b, iteration, token)
        if (b, iteration, stage) == (0, 0, back):
            slots, turned, order = load(False, blocks, (token,), [ANY], {})
            slots, turned, order = load(
                True, partner, (others[0], slots, turned), [VMEM, ANY, ANY], {3: 0, 4: 1}
            )
        if (b, iteration, stage) == (1, 0, forward):
            floor, *held = call(
                rows_kernel,
                (shape(1, rows),) + (shape(size, rows),) * (2 * BATCHES),
                [SMEM] + [HBM] * 2 + [ANY] * 2 + [VMEM] * 2 + [ANY],
                [pltpu.VMEM((2 * rows, width), f32), pltpu.SemaphoreType.DMA((2,))],
                name="turn_rows",
            )(place, *sides, vectors_in[-1], others[0], token)
            dual, right = held[:BATCHES], held[BATCHES:]
        if (b, iteration, stage) == (BATCHES - 1, ITERS - 1, pair):
            primal_final, token = call(
                primal_out_kernel,
                (pltpu.HBM((cols, profiles), f32), shape(8, TAIL)),
                [SMEM] + [VMEM] * (2 * BATCHES) + [ANY],
                name="primal_out",
            )(place, *primal, *[to_core(p) for p in primal], token)

    def last_operands(b):
        return place, dual[b], *steps[b], halves[b][1], partner_before[b]

    part = call(
        dual_part_kernel, shape(rows, width), [SMEM] + [VMEM] * 5 + [ANY], flops=STAGE_FLOPS, name="dual_part"
    )(*last_operands(0), token)
    dual_final = call(
        dual_out_kernel,
        pltpu.HBM((rows, profiles), f32),
        [SMEM] + [VMEM] * 6,
        [pltpu.VMEM((rows, profiles), f32), pltpu.SemaphoreType.DMA((4,))],
        name="dual_out",
        out_specs=HBM,
    )(*last_operands(1), part)
    return primal_final, dual_final


def solution(mesh):
    return jax.shard_map(
        local,
        mesh=mesh,
        in_specs=(
            P("row", "col"),
            P("row", "col"),
            P("col"),
            P("col"),
            P("col"),
            P("row"),
            P("col"),
            P("row", "groups"),
            P("col", "groups"),
            P("row", "groups"),
            P("groups"),
        ),
        out_specs=(P("col", "groups"), P("row", "groups")),
        check_vma=False,
    )
```
